256 devices in a mesh: pts: 64 (over z, x, core), grp: 4 (over y).
Axes of the slice: x: 4, y: 4, z: 8, core: 2. Of those that a mesh axis runs over, the one named last changes fastest.
Arguments:
- feats: bfloat16 [262144, 256], P(('pts', 'grp')), may hold values from -8 to 8
- counts: int32 [256], P(('pts', 'grp')), may hold values from 512 to 1024, as said below
- parent: int32 [262144], P(('pts', 'grp')), may hold values from 0 to 65535, as said below
- ln_gain: float32 [256], replicated, may hold values from 0.5 to 1.5
- w_qkv: bfloat16 [256, 768], replicated, may hold values from -0.41015625 to 0.41015625
- w_out: bfloat16 [256, 256], replicated, may hold values from -0.375 to 0.375
- w_down: bfloat16 [256, 512], replicated, may hold values from -0.375 to 0.375
- w_up: bfloat16 [512, 256], replicated, may hold values from -0.25 to 0.25
- cotangent: bfloat16 [262144, 256], P(('pts', 'grp')), may hold values from -6 to 6
Outputs:
- result: bfloat16 [262144, 256], P(('pts', 'grp'))
- d_feats: bfloat16 [262144, 256], P(('pts', 'grp'))
- grad_qkv: float32 [256, 768], replicated
- grad_out: float32 [256, 256], replicated
- grad_down: float32 [256, 512], replicated
- grad_up: float32 [512, 256], replicated
The draws below stay inside these ranges and needn't reach their ends.
Inputs may be any that keep to these rules, and one draw needn't show every extreme that they name: `counts`: the device holding the most live points holds 1024 of them; every device holds at least 512. `parent`: within each device's 1024 rows parents never fall. A live row of device d names a coarse row from d * 256 to d * 256 + 320 - 1 (the last device: its own 256 rows only), and its last live row names the last of these.
All inputs are finite; a program needn't handle non-finite values.
Results may differ from the reference program's by a relative error of at most 0.012.
The reference program's roundings to bfloat16 on the way count: a program that leaves them out, or rounds other values in their place, can miss the bound.
Values may be sent and summed in bfloat16 or wider, within the bound.
A program may use at most 64 MiB of HBM per device.

```python
import jax
import jax.numpy as jnp
from jax import lax

C1 = 256
C2 = 512
HD = 16
PATCH = 1024
SPILL = 64
HGROUP = 2
F_DEV = 1024
C_DEV = 256
SHARDS = 256
NF = 262144
NC = 65536


def count_table(key):
    key_a = jax.random.fold_in(key, 101)
    key_b = jax.random.fold_in(key, 102)
    raw = jax.random.randint(key_a, (SHARDS,), F_DEV - PATCH // 2, F_DEV + 1)
    fullest = jax.random.randint(key_b, (), 0, SHARDS)
    return jnp.where(jnp.arange(SHARDS) == fullest, F_DEV, raw).astype(jnp.int32)


def draw_feats(key, part):
    key = jax.random.fold_in(key, 3)
    key_noise = jax.random.fold_in(key, 0)
    values = jnp.clip(jax.random.normal(key_noise, (NF, C1), jnp.float32), -6.0, 6.0)
    return values.astype(jnp.bfloat16)


def draw_w_qkv(key, part):
    key = jax.random.fold_in(key, 4)
    limit = 6.0 * C1 ** (-0.5)
    base = jnp.clip(jax.random.normal(key, (C1, 3 * C1), jnp.float32) * C1 ** (-0.5), -limit, limit)
    return base.astype(jnp.bfloat16)


def draw_counts(key, part):
    table = count_table(key)
    return table


def draw_parent(key, part):
    table = count_table(key)
    key = jax.random.fold_in(key, 2)
    device_ids = jnp.arange(SHARDS, dtype=jnp.int32)[:, None]
    upper = jnp.where(device_ids == SHARDS - 1, C_DEV, C_DEV + SPILL).astype(jnp.int32)
    raw = jax.random.randint(key, (SHARDS, F_DEV), 0, upper)
    ordered = jnp.sort(raw, axis=1)
    position = jnp.arange(F_DEV, dtype=jnp.int32)[None, :]
    ordered = jnp.where(position >= table[:, None] - 1, upper - 1, ordered)
    return (device_ids * C_DEV + ordered).reshape(NF).astype(jnp.int32)


def level_of(own_key, shape, cuts, least, largest):
    loudness = 1.0
    for dim, blocks in cuts:
        draws = jax.random.uniform(jax.random.fold_in(jax.random.fold_in(own_key, 6), dim), (blocks,), jnp.float32, least / len(cuts), largest / len(cuts))
        loudness = loudness * jnp.repeat(jnp.exp(draws), shape[dim] // blocks).reshape((-1,) + (1,) * (len(shape) - 1 - dim))
    return loudness


def bell_draw(own_key, dims, scale, bound, cuts=(), kind=jnp.bfloat16):
    drawn = jax.random.normal(own_key, dims, jnp.float32) * scale
    if len(cuts) > 0:
        drawn = level_of(own_key, dims, cuts, -0.22, 0.18) * drawn
    return jnp.clip(drawn, min=-bound, max=bound).astype(kind)


def setup_inputs(seed: int = 0) -> dict:
    streams_of = jax.random.split(jax.random.key(seed), 10)
    feats = draw_feats(jax.random.fold_in(streams_of[9], 71), 0)
    counts = draw_counts(jax.random.fold_in(streams_of[9], 71), 0)
    parent = draw_parent(jax.random.fold_in(streams_of[9], 71), 0)
    ln_gain = jnp.clip(1.0 + 0.1 * jax.random.normal(streams_of[3], (C1,), jnp.float32), 0.5, 1.5)
    w_qkv = draw_w_qkv(jax.random.fold_in(streams_of[9], 71), 0)
    w_out = bell_draw(streams_of[5], (C1, C1), C1 ** -0.5, 0.375)
    w_down = bell_draw(streams_of[6], (C1, C2), C1 ** -0.5, 0.375)
    w_up = bell_draw(streams_of[7], (C2, C1), C2 ** -0.5, 0.25)
    cotangent = bell_draw(streams_of[8], (NF, C1), 1.0, 6.0, ((0, 256),))
    return {"feats": feats, "counts": counts, "parent": parent, "ln_gain": ln_gain, "w_qkv": w_qkv, "w_out": w_out, "w_down": w_down, "w_up": w_up, "cotangent": cotangent}


def layer_norm(values, ln_gain):
    center = values - lax.optimization_barrier(jnp.mean(values, axis=-1, keepdims=True))
    spread = lax.optimization_barrier(jnp.mean(center * center, axis=-1, keepdims=True))
    return center * lax.rsqrt(spread + 1e-05) * ln_gain

def attend(query, keys, values, key_live):
    scores = jnp.einsum('grd,gsd->grs', query.astype(jnp.float32), keys.astype(jnp.float32)) * HD ** (-0.5)
    scores = jnp.where(key_live[None, None, :], scores, -1e+30)
    highest = lax.optimization_barrier(jnp.max(scores, axis=-1, keepdims=True))
    raised = jnp.exp(scores - highest)
    probs = (raised / lax.optimization_barrier(jnp.sum(raised, axis=-1, keepdims=True))).astype(jnp.bfloat16)
    mixed = jnp.einsum('grs,gsd->grd', probs.astype(jnp.float32), values.astype(jnp.float32))
    return mixed.astype(jnp.bfloat16)

def heads_first(block, width):
    return block.reshape(block.shape[0], width // (HGROUP * HD), HGROUP, HD).transpose(1, 2, 0, 3)

def heads_last(block):
    return block.transpose(2, 0, 1, 3).reshape(block.shape[2], -1)

def split_parts(proj_rows):
    width = proj_rows.shape[1] // 3
    query = heads_first(proj_rows[:, :width], width)
    keys = heads_first(proj_rows[:, width:2 * width], width)
    values = heads_first(proj_rows[:, 2 * width:], width)
    return (query, keys, values, width)

def patch_forward(proj_rows, key_live):
    query, keys, values, width = split_parts(proj_rows)

    def one_group(group):
        return attend(group[0], group[1], group[2], key_live)
    return heads_last(lax.map(one_group, (query, keys, values)))

def patch_backward(proj_rows, key_live, d_attended):
    query, keys, values, width = split_parts(proj_rows)
    d_heads = heads_first(d_attended, width)

    def one_group(group):

        def inner(query_g, keys_g, values_g):
            return attend(query_g, keys_g, values_g, key_live)
        _, pull = jax.vjp(inner, group[0], group[1], group[2])
        return pull(group[3])
    d_query, d_keys, d_values = lax.map(one_group, (query, keys, values, d_heads))
    return jnp.concatenate([heads_last(d_query), heads_last(d_keys), heads_last(d_values)], axis=1)

def reference(feats, counts, parent, ln_gain, w_qkv, w_out, w_down, w_up, cotangent):
    row_ids = jnp.arange(NF, dtype=jnp.int32)
    live_rows = row_ids % F_DEV < jnp.repeat(counts, F_DEV)
    weight = live_rows.astype(jnp.float32)
    feats_wide = feats.astype(jnp.float32)
    normed = layer_norm(feats_wide, ln_gain).astype(jnp.bfloat16)
    proj = jnp.dot(normed, w_qkv, preferred_element_type=jnp.float32).astype(jnp.bfloat16)
    proj_patches = proj.reshape(NF // PATCH, PATCH, 3 * C1)
    key_live = live_rows.reshape(NF // PATCH, PATCH)

    def forward_one(pair):
        return patch_forward(pair[0], pair[1])
    attended = lax.map(forward_one, (proj_patches, key_live)).reshape(NF, C1)
    hidden = (feats_wide + jnp.dot(attended, w_out, preferred_element_type=jnp.float32)).astype(jnp.bfloat16)
    pooled_sum = jax.ops.segment_sum(hidden.astype(jnp.float32) * weight[:, None], parent, num_segments=NC)
    child_count = jax.ops.segment_sum(weight, parent, num_segments=NC)
    denominator = jnp.maximum(child_count, 1.0)
    pooled = (pooled_sum / denominator[:, None]).astype(jnp.bfloat16)
    pre = jnp.dot(pooled, w_down, preferred_element_type=jnp.float32)
    activ = jax.nn.gelu(pre).astype(jnp.bfloat16)
    back = jnp.dot(activ, w_up, preferred_element_type=jnp.float32).astype(jnp.bfloat16)
    unpooled = jnp.where(live_rows[:, None], back[parent].astype(jnp.float32), 0.0)
    result = (hidden.astype(jnp.float32) + unpooled).astype(jnp.bfloat16)
    d_back = jax.ops.segment_sum(cotangent.astype(jnp.float32) * weight[:, None], parent, num_segments=NC).astype(jnp.bfloat16)
    d_gelu = jnp.dot(d_back, w_up.T, preferred_element_type=jnp.float32)
    _, gelu_pull = jax.vjp(jax.nn.gelu, pre)
    d_pre = gelu_pull(d_gelu)[0].astype(jnp.bfloat16)
    grad_up = jnp.dot(activ.T, d_back, preferred_element_type=jnp.float32)
    grad_down = jnp.dot(pooled.T, d_pre, preferred_element_type=jnp.float32)
    d_share = jnp.dot(d_pre, w_down.T, preferred_element_type=jnp.float32) / denominator[:, None]
    d_hidden = cotangent.astype(jnp.float32) + jnp.where(live_rows[:, None], d_share[parent], 0.0)
    d_hidden_b = d_hidden.astype(jnp.bfloat16)
    grad_out = jnp.dot(attended.T, d_hidden_b, preferred_element_type=jnp.float32)
    d_attended = jnp.dot(d_hidden_b, w_out.T, preferred_element_type=jnp.float32).astype(jnp.bfloat16)

    def backward_one(triple):
        return patch_backward(triple[0], triple[1], triple[2])
    d_proj = lax.map(backward_one, (proj_patches, key_live, d_attended.reshape(NF // PATCH, PATCH, C1))).reshape(NF, 3 * C1)
    grad_qkv = jnp.dot(normed.T, d_proj, preferred_element_type=jnp.float32)
    d_normed = jnp.dot(d_proj, w_qkv.T, preferred_element_type=jnp.float32)

    def norm_only(values):
        return layer_norm(values, ln_gain)
    _, norm_pull = jax.vjp(norm_only, feats_wide)
    d_feats = (d_hidden + norm_pull(d_normed)[0]).astype(jnp.bfloat16)
    return (result, d_feats, grad_qkv, grad_out, grad_down, grad_up)
```

```python
import functools

import jax
import jax.numpy as jnp
from jax import lax
from jax.experimental import pallas as pl
from jax.experimental.pallas import tpu as pltpu
from jax.sharding import PartitionSpec as P

HD = 16
HEADS = 16
ROWS = 1024
C1 = 256
C2 = 512
CORE = 256
SPILL = 64
TABLE = CORE + SPILL
PAIR = 2
STEPS = HEADS // PAIR
HALF = 128
SAFE_SCORE = 60.0
MESH = pl.DeviceIdType.MESH
BF = jnp.bfloat16
F32 = jnp.float32


def dg(left, right, left_dim, right_dim):
    return lax.dot_general(
        left,
        right,
        (((left_dim,), (right_dim,)), ((), ())),
        preferred_element_type=F32,
    )


def iota(shape, dim):
    return lax.broadcasted_iota(jnp.int32, shape, dim)


def norm_parts(wide):
    center = wide - jnp.mean(wide, axis=-1, keepdims=True)
    spread = jnp.mean(center * center, axis=-1, keepdims=True)
    inverse = lax.rsqrt(spread + 1e-05)
    return center * inverse, inverse


def device_number():
    return lax.axis_index("pts") * lax.axis_size("grp") + lax.axis_index("grp")


def whole(shape):
    return pl.BlockSpec(shape, lambda i, n=len(shape): (0,) * n)


def per_pair(rows):
    return pl.BlockSpec((PAIR, rows, ROWS), lambda i: (i, 0, 0))


def forward_kernel(
    counts_ref, parent_ref, feats_ref, gain_ref, w_qkv_ref, w_out_ref, cot_ref,
    raised_ref, proj_ref, scale_ref, att_ref, hidden_ref, sum_ref, count_ref, cot_sum_ref,
    keys_s, query_s, values_s, mixed_s, safe_s,
):
    step = pl.program_id(0)
    live = counts_ref[0]

    @pl.when(step == 0)
    def _():
        xhat, _ = norm_parts(feats_ref[...].astype(F32))
        normed = (xhat * gain_ref[...]).astype(BF)
        proj = dg(w_qkv_ref[...], normed, 0, 1).astype(BF)
        proj_ref[...] = proj
        keys = dg(normed, w_qkv_ref[:, C1 : 2 * C1], 1, 0).astype(BF)
        dead = (iota((ROWS, HALF), 0) >= live) & (iota((ROWS, HALF), 1) == 0)
        bias = jnp.where(dead, -1e30, 0.0).astype(BF)
        for half in range(2):
            keys_s[half, :, :HALF] = keys[:, half * HALF : (half + 1) * HALF]
            keys_s[half, :, HALF:] = bias
        ones = jnp.where(iota((HALF, ROWS), 0) == 0, 1.0, 0.0).astype(BF)
        for one in range(PAIR):
            query_s[one, HALF:, :] = ones
            values_s[one, HD:, :] = jnp.ones((HD, ROWS), BF)
        wide = proj[: 2 * C1, :].astype(F32)
        squares = jnp.sum((wide * wide).reshape(2, HEADS, HD, ROWS), axis=2)
        bound = jnp.max(squares[0]) * jnp.max(squares[1]) / HD
        safe_s[0] = (bound <= SAFE_SCORE * SAFE_SCORE).astype(jnp.int32)

    half = step // (STEPS // 2)
    for one in range(PAIR):
        head = step * PAIR + one
        start = pl.multiple_of(head * HD, HD)
        place = pl.multiple_of(lax.rem(head, HEADS // 2) * HD, HD)
        query_s[one, :HALF, :] = jnp.zeros((HALF, ROWS), BF)
        query_s[one, pl.ds(place, HD), :] = proj_ref[pl.ds(start, HD), :] * jnp.asarray(
            HD ** (-0.5), BF
        )
        values_s[one, :HD, :] = proj_ref[pl.ds(2 * C1 + start, HD), :]

    @pl.when(safe_s[0] == 1)
    def _():
        for one in range(PAIR):
            raised = jnp.exp(dg(keys_s[half], query_s[one], 1, 0)).astype(BF)
            raised_ref[one] = raised
            mixed_s[one] = dg(values_s[one], raised, 1, 0)

    @pl.when(safe_s[0] != 1)
    def _():
        for one in range(PAIR):
            scores = dg(keys_s[half], query_s[one], 1, 0)
            highest = jnp.max(scores, axis=0, keepdims=True)
            raised = jnp.exp(scores - highest).astype(BF)
            raised_ref[one] = raised
            mixed_s[one] = dg(values_s[one], raised, 1, 0)

    for one in range(PAIR):
        start = pl.multiple_of((step * PAIR + one) * HD, HD)
        scale = 1.0 / mixed_s[one, HD:, :]
        att_ref[pl.ds(start, HD), :] = (mixed_s[one, :HD, :] * scale).astype(BF)
        scale_ref[one] = scale[:8]

    @pl.when(step == STEPS - 1)
    def _():
        attended = att_ref[...].T
        hidden = (
            feats_ref[...].astype(F32) + dg(attended, w_out_ref[...], 1, 0)
        ).astype(BF)
        hidden_ref[...] = hidden
        local = parent_ref[...] - device_number() * CORE
        member = (local == iota((TABLE, ROWS), 0)) & (iota((TABLE, ROWS), 1) < live)
        member_f = jnp.where(member, 1.0, 0.0)
        count_ref[...] = jnp.broadcast_to(
            jnp.sum(member_f, axis=1, keepdims=True), (TABLE, HALF)
        )
        member_b = member_f.astype(BF)
        sum_ref[...] = dg(member_b, hidden, 1, 0)
        cot_sum_ref[...] = dg(member_b, cot_ref[...], 1, 0)


def forward_call(counts, parent, feats, gain, w_qkv, w_out, cotangent):
    out = jax.ShapeDtypeStruct
    return pl.pallas_call(
        forward_kernel,
        grid=(STEPS,),
        in_specs=[
            pl.BlockSpec(memory_space=pltpu.SMEM),
            whole((1, ROWS)),
            whole((ROWS, C1)),
            whole((1, C1)),
            whole((C1, 3 * C1)),
            whole((C1, C1)),
            whole((ROWS, C1)),
        ],
        out_specs=[
            per_pair(ROWS),
            whole((3 * C1, ROWS)),
            per_pair(8),
            whole((C1, ROWS)),
            whole((ROWS, C1)),
            whole((TABLE, C1)),
            whole((TABLE, HALF)),
            whole((TABLE, C1)),
        ],
        out_shape=[
            out((HEADS, ROWS, ROWS), BF),
            out((3 * C1, ROWS), BF),
            out((HEADS, 8, ROWS), F32),
            out((C1, ROWS), BF),
            out((ROWS, C1), BF),
            out((TABLE, C1), F32),
            out((TABLE, HALF), F32),
            out((TABLE, C1), F32),
        ],
        scratch_shapes=[
            pltpu.VMEM((2, ROWS, C1), BF),
            pltpu.VMEM((PAIR, C1, ROWS), BF),
            pltpu.VMEM((PAIR, 2 * HD, ROWS), BF),
            pltpu.VMEM((PAIR, 2 * HD, ROWS), F32),
            pltpu.SMEM((1,), jnp.int32),
        ],
        compiler_params=pltpu.CompilerParams(vmem_limit_bytes=56 * 2**20),
        name="forward",
    )(counts, parent, feats, gain, w_qkv, w_out, cotangent)


def gelu_and_slope(pre):
    root = 0.7978845608028654
    square = pre * pre
    tanh = jnp.tanh(root * (pre + 0.044715 * (square * pre)))
    value = pre * (0.5 * (1.0 + tanh))
    slope = 0.5 * (1.0 + tanh) + 0.5 * pre * (1.0 - tanh * tanh) * root * (
        1.0 + 3 * 0.044715 * square
    )
    return value, slope


def neighbour(distance):
    devices = lax.axis_size("pts") * lax.axis_size("grp")
    other = lax.rem(device_number() + distance + devices, devices)
    return (other // lax.axis_size("grp"), lax.rem(other, lax.axis_size("grp")))


def coarse_kernel(
    sum_ref, count_ref, cot_sum_ref, w_down_ref, w_up_ref,
    back_ref, share_ref, low_ref, grad_up_ref, grad_down_ref,
    send_up, recv_up, send_down, recv_down, send_sem, recv_sem,
):
    after, before = neighbour(1), neighbour(-1)
    barrier = pltpu.get_barrier_semaphore()
    for other in (after, before):
        pl.semaphore_signal(barrier, inc=1, device_id=other, device_id_type=MESH)
    send_up[:, :C1] = sum_ref[CORE:, :].astype(BF)
    send_up[:, C1 : 2 * C1] = cot_sum_ref[CORE:, :].astype(BF)
    spilled = count_ref[CORE:, :]
    high = spilled.astype(BF)
    low = (spilled - high.astype(F32)).astype(BF)
    send_up[:, 2 * C1 :] = jnp.where(iota((SPILL, HALF), 1) < HALF // 2, high, low)
    pl.semaphore_wait(barrier, 2)
    up = pltpu.make_async_remote_copy(
        send_up, recv_up, send_sem.at[0], recv_sem.at[0],
        device_id=after, device_id_type=MESH,
    )
    up.start()
    up.wait()
    got = recv_up[...].astype(F32)
    count_in = got[:, 2 * C1 : 2 * C1 + 1] + got[:, 2 * C1 + HALF // 2 : 2 * C1 + HALF // 2 + 1]
    own_sum = jnp.concatenate([sum_ref[:SPILL, :] + got[:, :C1], sum_ref[SPILL:CORE, :]], axis=0)
    own_cot = jnp.concatenate(
        [cot_sum_ref[:SPILL, :] + got[:, C1 : 2 * C1], cot_sum_ref[SPILL:CORE, :]], axis=0
    )
    counted = jnp.concatenate(
        [count_ref[:SPILL, :1] + count_in, count_ref[SPILL:CORE, :1]], axis=0
    )
    inverse = 1.0 / jnp.maximum(counted, 1.0)
    pooled = (own_sum * inverse).astype(BF)
    pre = dg(pooled, w_down_ref[...], 1, 0)
    value, slope = gelu_and_slope(pre)
    activ = value.astype(BF)
    back = dg(activ, w_up_ref[...], 1, 0).astype(BF)
    d_back = own_cot.astype(BF)
    d_pre = (dg(d_back, w_up_ref[...], 1, 1) * slope).astype(BF)
    share = dg(d_pre, w_down_ref[...], 1, 1) * inverse
    share_high = share.astype(BF)
    send_down[:, :C1] = back[:SPILL, :]
    send_down[:, C1:] = share_high[:SPILL, :]
    down = pltpu.make_async_remote_copy(
        send_down, recv_down, send_sem.at[1], recv_sem.at[1],
        device_id=before, device_id_type=MESH,
    )
    down.start()
    back_ref[:CORE, :] = back
    share_ref[:CORE, :] = share_high
    low_ref[:CORE, :] = (share - share_high.astype(F32)).astype(BF)
    low_ref[CORE:, :] = jnp.zeros((SPILL, C1), BF)
    grad_up_ref[...] = dg(activ, d_back, 0, 0)
    grad_down_ref[...] = dg(pooled, d_pre, 0, 0)
    down.wait()
    back_ref[CORE:, :] = recv_down[:, :C1]
    share_ref[CORE:, :] = recv_down[:, C1:]


def coarse_call(sums, counted, cot_sums, w_down, w_up):
    out = jax.ShapeDtypeStruct
    vmem = pl.BlockSpec(memory_space=pltpu.VMEM)
    return pl.pallas_call(
        coarse_kernel,
        in_specs=[vmem] * 5,
        out_specs=[vmem] * 5,
        out_shape=[
            out((TABLE, C1), BF),
            out((TABLE, C1), BF),
            out((TABLE, C1), BF),
            out((C2, C1), F32),
            out((C1, C2), F32),
        ],
        scratch_shapes=[
            pltpu.VMEM((SPILL, 2 * C1 + HALF), BF),
            pltpu.VMEM((SPILL, 2 * C1 + HALF), BF),
            pltpu.VMEM((SPILL, 2 * C1), BF),
            pltpu.VMEM((SPILL, 2 * C1), BF),
            pltpu.SemaphoreType.DMA((2,)),
            pltpu.SemaphoreType.DMA((2,)),
        ],
        compiler_params=pltpu.CompilerParams(
            collective_id=0, has_side_effects=True, vmem_limit_bytes=48 * 2**20
        ),
        name="coarse",
    )(sums, counted, cot_sums, w_down, w_up)


def backward_kernel(
    counts_ref, parent_ref, feats_ref, gain_ref, w_qkv_ref, w_out_ref, cot_ref,
    hidden_ref, att_ref, proj_ref, scale_ref, back_ref, share_ref, low_ref, raised_ref,
    result_ref, d_feats_ref, grad_qkv_ref, grad_out_ref,
    d_hidden_s, normed_s, d_att_s, d_proj_s, values_s, cots_s,
):
    step = pl.program_id(0)
    live = counts_ref[0]

    @pl.when(step == 0)
    def _():
        xhat, _ = norm_parts(feats_ref[...].astype(F32))
        normed = (xhat * gain_ref[...]).astype(BF)
        normed_s[...] = normed
        values = dg(normed, w_qkv_ref[:, 2 * C1 :], 1, 0).astype(BF)
        ones = jnp.where(iota((ROWS, HALF), 1) < 2, 1.0, 0.0).astype(BF)
        for half in range(2):
            values_s[half, :, :HALF] = values[:, half * HALF : (half + 1) * HALF]
            values_s[half, :, HALF:] = ones
        for one in range(PAIR):
            cots_s[one] = jnp.zeros((C1, ROWS), BF)
        local = parent_ref[...] - device_number() * CORE
        column = jnp.broadcast_to(local.astype(F32), (HALF, ROWS)).T[:, :1].astype(jnp.int32)
        member = (column == iota((ROWS, TABLE), 1)) & (iota((ROWS, TABLE), 0) < live)
        member_b = jnp.where(member, 1.0, 0.0).astype(BF)
        result_ref[...] = (
            hidden_ref[...].astype(F32) + dg(member_b, back_ref[...], 1, 0)
        ).astype(BF)
        d_hidden = (
            cot_ref[...].astype(F32)
            + dg(member_b, share_ref[...], 1, 0)
            + dg(member_b, low_ref[...], 1, 0)
        )
        d_hidden_s[...] = d_hidden
        d_hidden_b = d_hidden.astype(BF)
        grad_out_ref[...] = dg(att_ref[...], d_hidden_b, 1, 0)
        d_att_s[...] = dg(w_out_ref[...], d_hidden_b, 1, 1).astype(BF)

    half = step // (STEPS // 2)
    quarter = jnp.asarray(HD ** (-0.5), BF)
    for one in range(PAIR):
        head = step * PAIR + one
        start = pl.multiple_of(head * HD, HD)
        place = pl.multiple_of(lax.rem(head, HEADS // 2) * HD, HD)
        cot = (d_att_s[pl.ds(start, HD), :].astype(F32) * scale_ref[one, :1, :]).astype(BF)
        inner = -jnp.sum(
            cot.astype(F32) * att_ref[pl.ds(start, HD), :].astype(F32), axis=0, keepdims=True
        )
        high = inner.astype(BF).astype(F32)
        rows = iota((HD, ROWS), 0)
        cots_s[one, :HALF, :] = jnp.zeros((HALF, ROWS), BF)
        cots_s[one, pl.ds(place, HD), :] = cot
        cots_s[one, HALF : HALF + HD, :] = jnp.where(
            rows == 0, high, jnp.where(rows == 1, inner - high, 0.0)
        ).astype(BF)
        raised = raised_ref[one]
        d_scores = raised * dg(values_s[half], cots_s[one], 1, 0).astype(BF)
        d_proj_s[pl.ds(start, HD), :] = dg(
            proj_ref[pl.ds(C1 + start, HD), :] * quarter, d_scores, 1, 0
        ).astype(BF)
        d_proj_s[pl.ds(2 * C1 + start, HD), :] = dg(cot, raised, 1, 1).astype(BF)
        d_proj_s[pl.ds(C1 + start, HD), :] = dg(
            proj_ref[pl.ds(start, HD), :] * quarter, d_scores, 1, 1
        ).astype(BF)

    @pl.when(step == STEPS - 1)
    def _():
        grad_qkv_ref[...] = dg(normed_s[...], d_proj_s[...], 0, 1)
        d_normed = dg(w_qkv_ref[...], d_proj_s[...], 1, 0).T
        xhat, inverse = norm_parts(feats_ref[...].astype(F32))
        grown = d_normed * gain_ref[...]
        along = jnp.mean(grown * xhat, axis=-1, keepdims=True)
        d_wide = inverse * (grown - jnp.mean(grown, axis=-1, keepdims=True) - xhat * along)
        d_feats_ref[...] = (d_hidden_s[...] + d_wide).astype(BF)


def backward_call(
    counts, parent, feats, gain, w_qkv, w_out, cotangent,
    hidden, att, proj, scale, back, share, low, raised,
):
    out = jax.ShapeDtypeStruct
    return pl.pallas_call(
        backward_kernel,
        grid=(STEPS,),
        in_specs=[
            pl.BlockSpec(memory_space=pltpu.SMEM),
            whole((1, ROWS)),
            whole((ROWS, C1)),
            whole((1, C1)),
            whole((C1, 3 * C1)),
            whole((C1, C1)),
            whole((ROWS, C1)),
            whole((ROWS, C1)),
            whole((C1, ROWS)),
            whole((3 * C1, ROWS)),
            per_pair(8),
            whole((TABLE, C1)),
            whole((TABLE, C1)),
            whole((TABLE, C1)),
            per_pair(ROWS),
        ],
        out_specs=[
            whole((ROWS, C1)),
            whole((ROWS, C1)),
            whole((C1, 3 * C1)),
            whole((C1, C1)),
        ],
        out_shape=[
            out((ROWS, C1), BF),
            out((ROWS, C1), BF),
            out((C1, 3 * C1), F32),
            out((C1, C1), F32),
        ],
        scratch_shapes=[
            pltpu.VMEM((ROWS, C1), F32),
            pltpu.VMEM((ROWS, C1), BF),
            pltpu.VMEM((C1, ROWS), BF),
            pltpu.VMEM((3 * C1, ROWS), BF),
            pltpu.VMEM((2, ROWS, C1), BF),
            pltpu.VMEM((PAIR, C1, ROWS), BF),
        ],
        compiler_params=pltpu.CompilerParams(vmem_limit_bytes=56 * 2**20),
        name="backward",
    )(
        counts, parent, feats, gain, w_qkv, w_out, cotangent,
        hidden, att, proj, scale, back, share, low, raised,
    )


def per_device(feats, counts, parent, ln_gain, w_qkv, w_out, w_down, w_up, cotangent):
    parent_row = parent.reshape(1, ROWS)
    gain = ln_gain.reshape(1, C1)
    raised, proj, scale, att, hidden, sums, counted, cot_sums = forward_call(
        counts, parent_row, feats, gain, w_qkv, w_out, cotangent
    )
    back, share, low, grad_up, grad_down = coarse_call(sums, counted, cot_sums, w_down, w_up)
    result, d_feats, grad_qkv, grad_out = backward_call(
        counts, parent_row, feats, gain, w_qkv, w_out, cotangent,
        hidden, att, proj, scale, back, share, low, raised,
    )
    grad_qkv, grad_out, grad_down, grad_up = lax.psum(
        (grad_qkv, grad_out, grad_down, grad_up), ("pts", "grp")
    )
    return (result, d_feats, grad_qkv, grad_out, grad_down, grad_up)


def solution(mesh):
    rows = P(("pts", "grp"), None)
    line = P(("pts", "grp"))
    return jax.shard_map(
        per_device,
        mesh=mesh,
        in_specs=(rows, line, line, P(), P(), P(), P(), P(), rows),
        out_specs=(rows, rows, P(), P(), P(), P()),
        check_vma=False,
    )
```

```python
import jax
import jax.numpy as jnp
from jax import lax
from jax.experimental import pallas as pl
from jax.experimental.pallas import tpu as pltpu
from jax.sharding import PartitionSpec as P

HD = 16
HEADS = 16
ROWS = 1024
C1 = 256
C2 = 512
CORE = 256
SPILL = 64
TABLE = CORE + SPILL
PAIR = 2
STEPS = HEADS // PAIR
HALF = 128
SAFE_SCORE = 60.0
MESH = pl.DeviceIdType.MESH
BF = jnp.bfloat16
F32 = jnp.float32


def dg(left, right, left_dim, right_dim):
    return lax.dot_general(
        left,
        right,
        (((left_dim,), (right_dim,)), ((), ())),
        preferred_element_type=F32,
    )


def iota(shape, dim):
    return lax.broadcasted_iota(jnp.int32, shape, dim)


def norm_parts(wide):
    center = wide - jnp.mean(wide, axis=-1, keepdims=True)
    spread = jnp.mean(center * center, axis=-1, keepdims=True)
    inverse = lax.rsqrt(spread + 1e-05)
    return center * inverse, inverse


def device_number():
    return lax.axis_index("pts") * lax.axis_size("grp") + lax.axis_index("grp")


def whole(shape):
    return pl.BlockSpec(shape, lambda i, n=len(shape): (0,) * n)


def per_pair(rows):
    return pl.BlockSpec((PAIR, rows, ROWS), lambda i: (i, 0, 0))


def forward_kernel(
    counts_ref, parent_ref, feats_ref, gain_ref, w_qkv_ref, w_out_ref, cot_ref,
    raised_ref, proj_ref, scale_ref, att_ref, hidden_ref, sum_ref, count_ref, cot_sum_ref,
    keys_s, query_s, values_s, mixed_s, safe_s,
):
    step = pl.program_id(0)
    live = counts_ref[0]

    @pl.when(step == 0)
    def _():
        xhat, _ = norm_parts(feats_ref[...].astype(F32))
        normed = (xhat * gain_ref[...]).astype(BF)
        proj = dg(w_qkv_ref[...], normed, 0, 1).astype(BF)
        proj_ref[...] = proj
        keys = dg(normed, w_qkv_ref[:, C1 : 2 * C1], 1, 0).astype(BF)
        dead = (iota((ROWS, HALF), 0) >= live) & (iota((ROWS, HALF), 1) == 0)
        bias = jnp.where(dead, -1e30, 0.0).astype(BF)
        for half in range(2):
            keys_s[half, :, :HALF] = keys[:, half * HALF : (half + 1) * HALF]
            keys_s[half, :, HALF:] = bias
        ones = jnp.where(iota((HALF, ROWS), 0) == 0, 1.0, 0.0).astype(BF)
        for one in range(PAIR):
            query_s[one, HALF:, :] = ones
            values_s[one, HD:, :] = jnp.ones((HD, ROWS), BF)
        wide = proj[: 2 * C1, :].astype(F32)
        squares = jnp.sum((wide * wide).reshape(2, HEADS, HD, ROWS), axis=2)
        bound = jnp.max(squares[0]) * jnp.max(squares[1]) / HD
        safe_s[0] = (bound <= SAFE_SCORE * SAFE_SCORE).astype(jnp.int32)

    half = step // (STEPS // 2)
    for one in range(PAIR):
        head = step * PAIR + one
        start = pl.multiple_of(head * HD, HD)
        place = pl.multiple_of(lax.rem(head, HEADS // 2) * HD, HD)
        query_s[one, :HALF, :] = jnp.zeros((HALF, ROWS), BF)
        query_s[one, pl.ds(place, HD), :] = proj_ref[pl.ds(start, HD), :] * jnp.asarray(
            HD ** (-0.5), BF
        )
        values_s[one, :HD, :] = proj_ref[pl.ds(2 * C1 + start, HD), :]

    @pl.when(safe_s[0] == 1)
    def _():
        for one in range(PAIR):
            raised = jnp.exp(dg(keys_s[half], query_s[one], 1, 0)).astype(BF)
            raised_ref[one] = raised
            mixed_s[one] = dg(values_s[one], raised, 1, 0)

    @pl.when(safe_s[0] != 1)
    def _():
        for one in range(PAIR):
            scores = dg(keys_s[half], query_s[one], 1, 0)
            highest = jnp.max(scores, axis=0, keepdims=True)
            raised = jnp.exp(scores - highest).astype(BF)
            raised_ref[one] = raised
            mixed_s[one] = dg(values_s[one], raised, 1, 0)

    for one in range(PAIR):
        start = pl.multiple_of((step * PAIR + one) * HD, HD)
        scale = 1.0 / mixed_s[one, HD:, :]
        att_ref[pl.ds(start, HD), :] = (mixed_s[one, :HD, :] * scale).astype(BF)
        scale_ref[one] = scale[:8]

    @pl.when(step == STEPS - 1)
    def _():
        attended = att_ref[...].T
        hidden = (
            feats_ref[...].astype(F32) + dg(attended, w_out_ref[...], 1, 0)
        ).astype(BF)
        hidden_ref[...] = hidden
        local = parent_ref[...] - device_number() * CORE
        member = (local == iota((TABLE, ROWS), 0)) & (iota((TABLE, ROWS), 1) < live)
        member_f = jnp.where(member, 1.0, 0.0)
        count_ref[...] = jnp.broadcast_to(
            jnp.sum(member_f, axis=1, keepdims=True), (TABLE, HALF)
        )
        member_b = member_f.astype(BF)
        sum_ref[...] = dg(member_b, hidden, 1, 0)
        cot_sum_ref[...] = dg(member_b, cot_ref[...], 1, 0)


def forward_call(counts, parent, feats, gain, w_qkv, w_out, cotangent):
    out = jax.ShapeDtypeStruct
    return pl.pallas_call(
        forward_kernel,
        grid=(STEPS,),
        in_specs=[
            pl.BlockSpec(memory_space=pltpu.SMEM),
            whole((1, ROWS)),
            whole((ROWS, C1)),
            whole((1, C1)),
            whole((C1, 3 * C1)),
            whole((C1, C1)),
            whole((ROWS, C1)),
        ],
        out_specs=[
            per_pair(ROWS),
            whole((3 * C1, ROWS)),
            per_pair(8),
            whole((C1, ROWS)),
            whole((ROWS, C1)),
            whole((TABLE, C1)),
            whole((TABLE, HALF)),
            whole((TABLE, C1)),
        ],
        out_shape=[
            out((HEADS, ROWS, ROWS), BF),
            out((3 * C1, ROWS), BF),
            out((HEADS, 8, ROWS), F32),
            out((C1, ROWS), BF),
            out((ROWS, C1), BF),
            out((TABLE, C1), F32),
            out((TABLE, HALF), F32),
            out((TABLE, C1), F32),
        ],
        scratch_shapes=[
            pltpu.VMEM((2, ROWS, C1), BF),
            pltpu.VMEM((PAIR, C1, ROWS), BF),
            pltpu.VMEM((PAIR, 2 * HD, ROWS), BF),
            pltpu.VMEM((PAIR, 2 * HD, ROWS), F32),
            pltpu.SMEM((1,), jnp.int32),
        ],
        compiler_params=pltpu.CompilerParams(vmem_limit_bytes=56 * 2**20),
        name="forward",
    )(counts, parent, feats, gain, w_qkv, w_out, cotangent)


def gelu_and_slope(pre):
    root = 0.7978845608028654
    square = pre * pre
    tanh = jnp.tanh(root * (pre + 0.044715 * (square * pre)))
    value = pre * (0.5 * (1.0 + tanh))
    slope = 0.5 * (1.0 + tanh) + 0.5 * pre * (1.0 - tanh * tanh) * root * (
        1.0 + 3 * 0.044715 * square
    )
    return value, slope


def neighbour(distance):
    devices = lax.axis_size("pts") * lax.axis_size("grp")
    other = lax.rem(device_number() + distance + devices, devices)
    return (other // lax.axis_size("grp"), lax.rem(other, lax.axis_size("grp")))


GROUP = 16
UP_W = 2 * C1 + HALF
EARLY_W = 2 * C1 + HALF
EARLY_ROW, FIRST_ROW, SECOND_ROW, THIRD_ROW = 0, 5, 10, 13
FIRST_W = 3 * HALF // 2
LATE_W = 3 * HALF // 2


class Places:
    def __init__(self):
        pts, self.y = lax.axis_index("pts"), lax.axis_index("grp")
        self.core = lax.rem(pts, 2)
        self.x = lax.rem(pts // 2, 4)
        self.z = pts // 8
        self.plane = self.x * 4 + self.y
        self.line = self.z * 2 + self.core

    def core_peer(self, j):
        return (self.z * 8 + self.x * 2 + j, self.y)

    def plane_peer(self, j):
        return (self.z * 8 + (j // 4) * 2 + self.core, lax.rem(j, 4))

    def column_peer(self, j):
        return (j * 8 + self.x * 2 + self.core, self.y)

    def line_peer(self, j):
        return ((j // 2) * 8 + self.x * 2 + lax.rem(j, 2), self.y)


class Exchange:
    def __init__(self, sems, row, members, me, peer, src, dst):
        self.send, self.recv = sems
        self.row, self.members, self.me, self.peer = row, members, me, peer
        self.src, self.dst = src, dst

    def other(self, k):
        return lax.rem(self.me + k, self.members)

    def copy(self, k, slot):
        return pltpu.make_async_remote_copy(
            self.src(self.other(k)),
            self.dst(slot),
            self.send.at[self.row, k],
            self.recv.at[self.row, slot],
            device_id=self.peer(self.other(k)),
            device_id_type=MESH,
        )

    def start(self):
        def one(k, carry):
            self.copy(k, self.me).start()
            return carry

        lax.fori_loop(1, self.members, one, 0)

    def wait(self):
        def one(k, carry):
            copy = self.copy(k, self.other(k))
            copy.wait_send()
            copy.wait_recv()
            return carry

        lax.fori_loop(1, self.members, one, 0)


def add_slots(first, ref, members, skip=None):
    def one(j, total):
        return total + ref[j].astype(F32)

    return lax.fori_loop(0, members, one, first)


class FiveStep:
    def __init__(self, places, sems, row, data, pair, half, got, line, full):
        core, plane = places.core, places.plane
        self.places, self.data, self.pair, self.half = places, data, pair, half
        self.got, self.line, self.full = got, line, full
        self.stages = [
            Exchange(sems, row, 2, core, places.core_peer,
                     lambda j: data.at[j], lambda s: pair.at[s]),
            Exchange(sems, row + 1, GROUP, plane, places.plane_peer,
                     lambda j: half.at[j], lambda s: got.at[s]),
            Exchange(sems, row + 2, 8, places.z, places.column_peer,
                     lambda j: line.at[places.z], lambda s: line.at[s]),
            Exchange(sems, row + 3, GROUP, plane, places.plane_peer,
                     lambda j: full.at[core, plane], lambda s: full.at[core, s]),
            Exchange(sems, row + 4, 2, core, places.core_peer,
                     lambda j: full.at[core], lambda s: full.at[s]),
        ]

    def begin(self):
        self.stages[0].start()

    def advance(self, stage):
        places = self.places
        core, plane = places.core, places.plane
        self.stages[stage].wait()
        if stage == 0:
            self.half[...] = (
                self.data[core].astype(F32) + self.pair[1 - core].astype(F32)
            ).astype(BF)
            self.got[plane] = self.half[plane]
        if stage == 1:
            zero = jnp.zeros(self.got.shape[1:], F32)
            self.line[places.z] = add_slots(zero, self.got, GROUP).astype(BF)
        if stage == 2:
            zero = jnp.zeros(self.got.shape[1:], F32)
            self.full[core, plane] = add_slots(zero, self.line, 8).astype(BF)
        if stage < 4:
            self.stages[stage + 1].start()


class ThreeStep:
    def __init__(self, places, sems, row, data, got, line, full):
        plane = places.plane
        self.places, self.data, self.got = places, data, got
        self.line, self.full = line, full
        self.stages = [
            Exchange(sems, row, GROUP, plane, places.plane_peer,
                     lambda j: data.at[j], lambda s: got.at[s]),
            Exchange(sems, row + 1, GROUP, places.line, places.line_peer,
                     lambda j: line.at[places.line], lambda s: line.at[s]),
            Exchange(sems, row + 2, GROUP, plane, places.plane_peer,
                     lambda j: full.at[plane], lambda s: full.at[s]),
        ]

    def begin(self):
        plane = self.places.plane
        self.stages[0].start()
        self.got[plane] = self.data[plane]

    def advance(self, stage):
        places = self.places
        self.stages[stage].wait()
        zero = jnp.zeros(self.got.shape[1:], F32)
        if stage == 0:
            self.line[places.line] = add_slots(zero, self.got, GROUP).astype(BF)
        if stage == 1:
            self.full[places.plane] = add_slots(zero, self.line, GROUP).astype(BF)
        if stage < 2:
            self.stages[stage + 1].start()


def backward_kernel(
    counts_ref, parent_ref, feats_ref, gain_ref, w_qkv_ref, w_out_ref, w_down_ref, w_up_ref,
    cot_ref, hidden_ref, att_ref, proj_ref, scale_ref, sum_ref, count_ref, cot_sum_ref,
    raised_ref,
    result_ref, d_feats_ref, early_ref, first_ref, second_ref, third_ref,
    d_hidden_s, normed_s, d_att_s, d_proj_s, values_s, cots_s, member_s, back_s,
    send_up, recv_up, send_down, recv_down,
    e_data, e_pair, e_half, e_got, e_line, e_full,
    f_data, f_pair, f_half, f_got, f_line, f_full,
    s_data, s_got, s_line, s_full,
    t_data, t_got, t_line, t_full,
    near_send, near_recv, far_send, far_recv,
):
    step = pl.program_id(0)
    live = counts_ref[0]
    places = Places()
    sems = (far_send, far_recv)
    early = FiveStep(places, sems, EARLY_ROW, e_data, e_pair, e_half, e_got, e_line, e_full)
    first = FiveStep(places, sems, FIRST_ROW, f_data, f_pair, f_half, f_got, f_line, f_full)
    second = ThreeStep(places, sems, SECOND_ROW, s_data, s_got, s_line, s_full)
    third = ThreeStep(places, sems, THIRD_ROW, t_data, t_got, t_line, t_full)

    @pl.when(step == 0)
    def _():
        after, before = neighbour(1), neighbour(-1)
        barrier = pltpu.get_barrier_semaphore()
        for other in (after, before):
            pl.semaphore_signal(barrier, inc=1, device_id=other, device_id_type=MESH)

        def greet(k, carry):
            for other in (
                places.plane_peer(lax.rem(places.plane + k, GROUP)),
                places.line_peer(lax.rem(places.line + k, GROUP)),
            ):
                pl.semaphore_signal(barrier, inc=1, device_id=other, device_id_type=MESH)
            return carry

        lax.fori_loop(1, GROUP, greet, 0)
        send_up[:, :C1] = sum_ref[CORE:, :].astype(BF)
        send_up[:, C1 : 2 * C1] = cot_sum_ref[CORE:, :].astype(BF)
        spilled = count_ref[CORE:, :]
        high = spilled.astype(BF)
        low = (spilled - high.astype(F32)).astype(BF)
        send_up[:, 2 * C1 :] = jnp.where(iota((SPILL, HALF), 1) < HALF // 2, high, low)
        pl.semaphore_wait(barrier, 2 * GROUP)
        up = pltpu.make_async_remote_copy(
            send_up, recv_up, near_send.at[0], near_recv.at[0],
            device_id=after, device_id_type=MESH,
        )
        up.start()

        xhat, _ = norm_parts(feats_ref[...].astype(F32))
        normed = (xhat * gain_ref[...]).astype(BF)
        normed_s[...] = normed
        values = dg(normed, w_qkv_ref[:, 2 * C1 :], 1, 0).astype(BF)
        ones = jnp.where(iota((ROWS, HALF), 1) < 2, 1.0, 0.0).astype(BF)
        for half in range(2):
            values_s[half, :, :HALF] = values[:, half * HALF : (half + 1) * HALF]
            values_s[half, :, HALF:] = ones
        for one in range(PAIR):
            cots_s[one] = jnp.zeros((C1, ROWS), BF)
        local = parent_ref[...] - device_number() * CORE
        column = jnp.broadcast_to(local.astype(F32), (HALF, ROWS)).T[:, :1].astype(jnp.int32)
        member = (column == iota((ROWS, TABLE), 1)) & (iota((ROWS, TABLE), 0) < live)
        member_s[...] = jnp.where(member, 1.0, 0.0).astype(BF)

        up.wait()
        got = recv_up[...].astype(F32)
        count_in = (
            got[:, 2 * C1 : 2 * C1 + 1] + got[:, 2 * C1 + HALF // 2 : 2 * C1 + HALF // 2 + 1]
        )
        own_sum = jnp.concatenate(
            [sum_ref[:SPILL, :] + got[:, :C1], sum_ref[SPILL:CORE, :]], axis=0
        )
        own_cot = jnp.concatenate(
            [cot_sum_ref[:SPILL, :] + got[:, C1 : 2 * C1], cot_sum_ref[SPILL:CORE, :]], axis=0
        )
        counted = jnp.concatenate(
            [count_ref[:SPILL, :1] + count_in, count_ref[SPILL:CORE, :1]], axis=0
        )
        inverse = 1.0 / jnp.maximum(counted, 1.0)
        pooled = (own_sum * inverse).astype(BF)
        pre = dg(pooled, w_down_ref[...], 1, 0)
        value, slope = gelu_and_slope(pre)
        activ = value.astype(BF)
        back = dg(activ, w_up_ref[...], 1, 0).astype(BF)
        d_back = own_cot.astype(BF)
        d_pre = (dg(d_back, w_up_ref[...], 1, 1) * slope).astype(BF)
        share = dg(d_pre, w_down_ref[...], 1, 1) * inverse
        share_high = share.astype(BF)
        send_down[:, :C1] = back[:SPILL, :]
        send_down[:, C1:] = share_high[:SPILL, :]
        down = pltpu.make_async_remote_copy(
            send_down, recv_down, near_send.at[1], near_recv.at[1],
            device_id=before, device_id_type=MESH,
        )
        down.start()
        share_low = (share - share_high.astype(F32)).astype(BF)
        grad_up = dg(activ, d_back, 0, 0).astype(BF)
        e_data[:, :, :, :C1] = grad_up.reshape(2, GROUP, 16, C1)
        grad_down = dg(pooled, d_pre, 0, 0).astype(BF).reshape(GROUP, 16, C2)
        for core in range(2):
            e_data[core, :, :, C1 : 2 * C1] = grad_down[:, :, core * C1 : (core + 1) * C1]
        back_s[:CORE, :] = back
        down.wait()
        back_s[CORE:, :] = recv_down[:, :C1]
        share_in = recv_down[:, C1:]
        member_b = member_s[...]
        d_hidden = (
            cot_ref[...].astype(F32)
            + dg(member_b, jnp.concatenate([share_high, share_in], axis=0), 1, 0)
            + dg(member_b[:, :CORE], share_low, 1, 0)
        )
        d_hidden_s[...] = d_hidden
        d_hidden_b = d_hidden.astype(BF)
        grad_out = dg(att_ref[...], d_hidden_b, 1, 0).astype(BF).reshape(GROUP, 16, C1)
        for core in range(2):
            e_data[core, :, :, 2 * C1 :] = grad_out[:, :, core * HALF : (core + 1) * HALF]
        early.begin()
        d_att_s[...] = dg(w_out_ref[...], d_hidden_b, 1, 1).astype(BF)

    for stage in range(5):
        @pl.when(step == stage + 1)
        def _(stage=stage):
            early.advance(stage)

    def grad_columns(start, width):
        return [
            dg(normed_s[...], d_proj_s[part * C1 + start : part * C1 + start + width, :], 0, 1)
            for part in range(3)
        ]

    @pl.when(step == 4)
    def _():
        grads = jnp.concatenate(grad_columns(0, HALF), axis=1).astype(BF)
        for core in range(2):
            f_data[core] = grads[:, core * FIRST_W : (core + 1) * FIRST_W].reshape(
                GROUP, 16, FIRST_W
            )
        first.begin()

    for stage in range(3):
        @pl.when(step == stage + 5)
        def _(stage=stage):
            first.advance(stage)

    @pl.when(step == 6)
    def _():
        grads = jnp.concatenate(grad_columns(HALF, HALF // 2), axis=1).astype(BF)
        s_data[...] = grads.reshape(GROUP, 16, LATE_W)
        second.begin()

    @pl.when(step == 7)
    def _():
        second.advance(0)

    half = step // (STEPS // 2)
    quarter = jnp.asarray(HD ** (-0.5), BF)
    for one in range(PAIR):
        head = step * PAIR + one
        start = pl.multiple_of(head * HD, HD)
        place = pl.multiple_of(lax.rem(head, HEADS // 2) * HD, HD)
        cot = (d_att_s[pl.ds(start, HD), :].astype(F32) * scale_ref[one, :1, :]).astype(BF)
        inner = -jnp.sum(
            cot.astype(F32) * att_ref[pl.ds(start, HD), :].astype(F32), axis=0, keepdims=True
        )
        high = inner.astype(BF).astype(F32)
        rows = iota((HD, ROWS), 0)
        cots_s[one, :HALF, :] = jnp.zeros((HALF, ROWS), BF)
        cots_s[one, pl.ds(place, HD), :] = cot
        cots_s[one, HALF : HALF + HD, :] = jnp.where(
            rows == 0, high, jnp.where(rows == 1, inner - high, 0.0)
        ).astype(BF)
        raised = raised_ref[one]
        d_scores = raised * dg(values_s[half], cots_s[one], 1, 0).astype(BF)
        d_proj_s[pl.ds(start, HD), :] = dg(
            proj_ref[pl.ds(C1 + start, HD), :] * quarter, d_scores, 1, 0
        ).astype(BF)
        d_proj_s[pl.ds(2 * C1 + start, HD), :] = dg(cot, raised, 1, 1).astype(BF)
        d_proj_s[pl.ds(C1 + start, HD), :] = dg(
            proj_ref[pl.ds(start, HD), :] * quarter, d_scores, 1, 1
        ).astype(BF)

    @pl.when(step == STEPS - 1)
    def _():
        grads = jnp.concatenate(grad_columns(HALF + HALF // 2, HALF // 2), axis=1).astype(BF)
        t_data[...] = grads.reshape(GROUP, 16, LATE_W)
        third.begin()
        first.advance(3)
        second.advance(1)
        d_normed = dg(w_qkv_ref[...], d_proj_s[...], 1, 0).T
        third.advance(0)
        xhat, inverse = norm_parts(feats_ref[...].astype(F32))
        grown = d_normed * gain_ref[...]
        along = jnp.mean(grown * xhat, axis=-1, keepdims=True)
        d_wide = inverse * (grown - jnp.mean(grown, axis=-1, keepdims=True) - xhat * along)
        d_feats_ref[...] = (d_hidden_s[...] + d_wide).astype(BF)
        third.advance(1)
        result_ref[...] = (
            hidden_ref[...].astype(F32) + dg(member_s[...], back_s[...], 1, 0)
        ).astype(BF)
        early_ref[...] = e_full[...]
        first.advance(4)
        first_ref[...] = f_full[...]
        second.advance(2)
        second_ref[...] = s_full[...]
        third.advance(2)
        third_ref[...] = t_full[...]


def backward_call(
    counts, parent, feats, gain, w_qkv, w_out, w_down, w_up, cotangent,
    hidden, att, proj, scale, sums, counted, cot_sums, raised,
):
    out = jax.ShapeDtypeStruct
    vmem = pltpu.VMEM
    early, first, late = (
        (2, GROUP, 16, EARLY_W), (2, GROUP, 16, FIRST_W), (GROUP, 16, LATE_W)
    )

    def five(shape):
        return [
            vmem(shape, BF), vmem(shape, BF), vmem(shape[1:], BF), vmem(shape[1:], BF),
            vmem((8,) + shape[2:], BF), vmem(shape, BF),
        ]

    return pl.pallas_call(
        backward_kernel,
        grid=(STEPS,),
        in_specs=[
            pl.BlockSpec(memory_space=pltpu.SMEM),
            whole((1, ROWS)),
            whole((ROWS, C1)),
            whole((1, C1)),
            whole((C1, 3 * C1)),
            whole((C1, C1)),
            whole((C1, C2)),
            whole((C2, C1)),
            whole((ROWS, C1)),
            whole((ROWS, C1)),
            whole((C1, ROWS)),
            whole((3 * C1, ROWS)),
            per_pair(8),
            whole((TABLE, C1)),
            whole((TABLE, HALF)),
            whole((TABLE, C1)),
            per_pair(ROWS),
        ],
        out_specs=[
            whole((ROWS, C1)),
            whole((ROWS, C1)),
            whole(early),
            whole(first),
            whole(late),
            whole(late),
        ],
        out_shape=[
            out((ROWS, C1), BF),
            out((ROWS, C1), BF),
            out(early, BF),
            out(first, BF),
            out(late, BF),
            out(late, BF),
        ],
        scratch_shapes=[
            vmem((ROWS, C1), F32),
            vmem((ROWS, C1), BF),
            vmem((C1, ROWS), BF),
            vmem((3 * C1, ROWS), BF),
            vmem((2, ROWS, C1), BF),
            vmem((PAIR, C1, ROWS), BF),
            vmem((ROWS, TABLE), BF),
            vmem((TABLE, C1), BF),
            vmem((SPILL, UP_W), BF),
            vmem((SPILL, UP_W), BF),
            vmem((SPILL, 2 * C1), BF),
            vmem((SPILL, 2 * C1), BF),
        ]
        + five(early)
        + five(first)
        + [vmem(late, BF)] * 8
        + [
            pltpu.SemaphoreType.DMA((2,)),
            pltpu.SemaphoreType.DMA((2,)),
            pltpu.SemaphoreType.DMA((16, GROUP)),
            pltpu.SemaphoreType.DMA((16, GROUP)),
        ],
        compiler_params=pltpu.CompilerParams(
            collective_id=0, has_side_effects=True, vmem_limit_bytes=58 * 2**20
        ),
        name="backward",
    )(
        counts, parent, feats, gain, w_qkv, w_out, w_down, w_up, cotangent,
        hidden, att, proj, scale, sums, counted, cot_sums, raised,
    )


def finish_kernel(
    result_ref, d_feats_ref, early_ref, first_ref, second_ref, third_ref,
    result_out, d_feats_out, qkv_out, out_out, down_out, up_out,
):
    result_out[...] = result_ref[...]
    d_feats_out[...] = d_feats_ref[...]
    for core in range(2):
        piece = early_ref[core]
        up_out[core * C1 : (core + 1) * C1, :] = piece[:, :, :C1].reshape(C1, C1).astype(F32)
        down_out[:, core * C1 : (core + 1) * C1] = (
            piece[:, :, C1 : 2 * C1].reshape(C1, C1).astype(F32)
        )
        out_out[:, core * HALF : (core + 1) * HALF] = (
            piece[:, :, 2 * C1 :].reshape(C1, HALF).astype(F32)
        )
    first = jnp.concatenate(
        [first_ref[core].reshape(C1, FIRST_W).astype(F32) for core in range(2)], axis=1
    )
    second = second_ref[...].reshape(C1, LATE_W).astype(F32)
    third = third_ref[...].reshape(C1, LATE_W).astype(F32)
    quarter = HALF // 2
    for part in range(3):
        base = part * C1
        qkv_out[:, base : base + HALF] = first[:, part * HALF : (part + 1) * HALF]
        qkv_out[:, base + HALF : base + C1] = jnp.concatenate(
            [
                second[:, part * quarter : (part + 1) * quarter],
                third[:, part * quarter : (part + 1) * quarter],
            ],
            axis=1,
        )


def finish_call(*parts):
    shapes = [
        ((ROWS, C1), BF), ((ROWS, C1), BF), ((C1, 3 * C1), F32), ((C1, C1), F32),
        ((C1, C2), F32), ((C2, C1), F32),
    ]
    return pl.pallas_call(
        finish_kernel,
        grid=(1,),
        in_specs=[whole(part.shape) for part in parts],
        out_specs=[whole(shape) for shape, _ in shapes],
        out_shape=[jax.ShapeDtypeStruct(shape, kind) for shape, kind in shapes],
        compiler_params=pltpu.CompilerParams(vmem_limit_bytes=32 * 2**20),
        name="finish",
    )(*parts)


def per_device(feats, counts, parent, ln_gain, w_qkv, w_out, w_down, w_up, cotangent):
    parent_row = parent.reshape(1, ROWS)
    gain = ln_gain.reshape(1, C1)
    raised, proj, scale, att, hidden, sums, counted, cot_sums = forward_call(
        counts, parent_row, feats, gain, w_qkv, w_out, cotangent
    )
    parts = backward_call(
        counts, parent_row, feats, gain, w_qkv, w_out, w_down, w_up, cotangent,
        hidden, att, proj, scale, sums, counted, cot_sums, raised,
    )
    return tuple(finish_call(*parts))


def solution(mesh):
    rows = P(("pts", "grp"), None)
    line = P(("pts", "grp"))
    return jax.shard_map(
        per_device,
        mesh=mesh,
        in_specs=(rows, line, line, P(), P(), P(), P(), P(), rows),
        out_specs=(rows, rows, P(), P(), P(), P()),
        check_vma=False,
    )
```

```python
import jax
import jax.numpy as jnp
from jax import lax
from jax.experimental import pallas as pl
from jax.experimental.pallas import tpu as pltpu
from jax.sharding import PartitionSpec as P

HD = 16
HEADS = 16
ROWS = 1024
C1 = 256
C2 = 512
CORE = 256
SPILL = 64
TABLE = CORE + SPILL
PAIR = 2
STEPS = HEADS // PAIR
HALF = 128
SAFE_SCORE = 60.0
MESH = pl.DeviceIdType.MESH
BF = jnp.bfloat16
F32 = jnp.float32


def dg(left, right, left_dim, right_dim):
    return lax.dot_general(
        left,
        right,
        (((left_dim,), (right_dim,)), ((), ())),
        preferred_element_type=F32,
    )


def iota(shape, dim):
    return lax.broadcasted_iota(jnp.int32, shape, dim)


def norm_parts(wide):
    center = wide - jnp.mean(wide, axis=-1, keepdims=True)
    spread = jnp.mean(center * center, axis=-1, keepdims=True)
    inverse = lax.rsqrt(spread + 1e-05)
    return center * inverse, inverse


def device_number():
    return lax.axis_index("pts") * lax.axis_size("grp") + lax.axis_index("grp")


def whole(shape):
    return pl.BlockSpec(shape, lambda i, n=len(shape): (0,) * n)


def per_pair(rows):
    return pl.BlockSpec((PAIR, rows, ROWS), lambda i: (i, 0, 0))


def forward_kernel(
    counts_ref, feats_ref, gain_ref, w_qkv_ref,
    raised_ref, proj_ref, scale_ref, att_ref,
    keys_s, query_s, values_s, mixed_s, safe_s,
):
    step = pl.program_id(0)
    live = counts_ref[0]

    @pl.when(step == 0)
    def _():
        xhat, _ = norm_parts(feats_ref[...].astype(F32))
        normed = (xhat * gain_ref[...]).astype(BF)
        proj = dg(w_qkv_ref[...], normed, 0, 1).astype(BF)
        proj_ref[...] = proj
        keys = dg(normed, w_qkv_ref[:, C1 : 2 * C1], 1, 0).astype(BF)
        dead = (iota((ROWS, HALF), 0) >= live) & (iota((ROWS, HALF), 1) == 0)
        bias = jnp.where(dead, -1e30, 0.0).astype(BF)
        for half in range(2):
            keys_s[half, :, :HALF] = keys[:, half * HALF : (half + 1) * HALF]
            keys_s[half, :, HALF:] = bias
        ones = jnp.where(iota((HALF, ROWS), 0) == 0, 1.0, 0.0).astype(BF)
        for one in range(PAIR):
            query_s[one, HALF:, :] = ones
            values_s[one, HD:, :] = jnp.ones((HD, ROWS), BF)
        wide = proj[: 2 * C1, :].astype(F32)
        squares = jnp.sum((wide * wide).reshape(2, HEADS, HD, ROWS), axis=2)
        bound = jnp.max(squares[0]) * jnp.max(squares[1]) / HD
        safe_s[0] = (bound <= SAFE_SCORE * SAFE_SCORE).astype(jnp.int32)

    half = step // (STEPS // 2)
    for one in range(PAIR):
        head = step * PAIR + one
        start = pl.multiple_of(head * HD, HD)
        place = pl.multiple_of(lax.rem(head, HEADS // 2) * HD, HD)
        query_s[one, :HALF, :] = jnp.zeros((HALF, ROWS), BF)
        query_s[one, pl.ds(place, HD), :] = proj_ref[pl.ds(start, HD), :] * jnp.asarray(
            HD ** (-0.5), BF
        )
        values_s[one, :HD, :] = proj_ref[pl.ds(2 * C1 + start, HD), :]

    @pl.when(safe_s[0] == 1)
    def _():
        for one in range(PAIR):
            raised = jnp.exp(dg(keys_s[half], query_s[one], 1, 0)).astype(BF)
            raised_ref[one] = raised
            mixed_s[one] = dg(values_s[one], raised, 1, 0)

    @pl.when(safe_s[0] != 1)
    def _():
        for one in range(PAIR):
            scores = dg(keys_s[half], query_s[one], 1, 0)
            highest = jnp.max(scores, axis=0, keepdims=True)
            raised = jnp.exp(scores - highest).astype(BF)
            raised_ref[one] = raised
            mixed_s[one] = dg(values_s[one], raised, 1, 0)

    for one in range(PAIR):
        start = pl.multiple_of((step * PAIR + one) * HD, HD)
        scale = 1.0 / mixed_s[one, HD:, :]
        att_ref[pl.ds(start, HD), :] = (mixed_s[one, :HD, :] * scale).astype(BF)
        scale_ref[one] = scale[:8]


def forward_call(counts, feats, gain, w_qkv):
    out = jax.ShapeDtypeStruct
    return pl.pallas_call(
        forward_kernel,
        grid=(STEPS,),
        in_specs=[
            pl.BlockSpec(memory_space=pltpu.SMEM),
            whole((ROWS, C1)),
            whole((1, C1)),
            whole((C1, 3 * C1)),
        ],
        out_specs=[
            per_pair(ROWS),
            whole((3 * C1, ROWS)),
            per_pair(8),
            whole((C1, ROWS)),
        ],
        out_shape=[
            out((HEADS, ROWS, ROWS), BF),
            out((3 * C1, ROWS), BF),
            out((HEADS, 8, ROWS), F32),
            out((C1, ROWS), BF),
        ],
        scratch_shapes=[
            pltpu.VMEM((2, ROWS, C1), BF),
            pltpu.VMEM((PAIR, C1, ROWS), BF),
            pltpu.VMEM((PAIR, 2 * HD, ROWS), BF),
            pltpu.VMEM((PAIR, 2 * HD, ROWS), F32),
            pltpu.SMEM((1,), jnp.int32),
        ],
        compiler_params=pltpu.CompilerParams(vmem_limit_bytes=56 * 2**20),
        name="forward",
    )(counts, feats, gain, w_qkv)


def gelu_and_slope(pre):
    root = 0.7978845608028654
    square = pre * pre
    tanh = jnp.tanh(root * (pre + 0.044715 * (square * pre)))
    value = pre * (0.5 * (1.0 + tanh))
    slope = 0.5 * (1.0 + tanh) + 0.5 * pre * (1.0 - tanh * tanh) * root * (
        1.0 + 3 * 0.044715 * square
    )
    return value, slope


def neighbour(distance):
    devices = lax.axis_size("pts") * lax.axis_size("grp")
    other = lax.rem(device_number() + distance + devices, devices)
    return (other // lax.axis_size("grp"), lax.rem(other, lax.axis_size("grp")))


GROUP = 16
UP_W = 2 * C1 + HALF
EARLY_W = 2 * C1 + HALF
EARLY_ROW, FIRST_ROW, SECOND_ROW, THIRD_ROW = 0, 5, 10, 15
FIRST_HEADS, SECOND_HEADS, THIRD_HEADS = 8, 4, 4
FIRST_W, SECOND_W, THIRD_W = (FIRST_HEADS * 24, SECOND_HEADS * 24, THIRD_HEADS * 48)
SERVICES = (
    (1, "early", 0), (5, "early", 1), (9, "early", 2), (13, "early", 3),
    (8, "first", -1), (9, "first", 0), (13, "first", 1),
    (12, "second", -1), (13, "second", 0),
)


class Places:
    def __init__(self):
        pts, self.y = lax.axis_index("pts"), lax.axis_index("grp")
        self.core = lax.rem(pts, 2)
        self.x = lax.rem(pts // 2, 4)
        self.z = pts // 8
        self.plane = self.x * 4 + self.y
        self.line = self.z * 2 + self.core

    def core_peer(self, j):
        return (self.z * 8 + self.x * 2 + j, self.y)

    def plane_peer(self, j):
        return (self.z * 8 + (j // 4) * 2 + self.core, lax.rem(j, 4))

    def column_peer(self, j):
        return (j * 8 + self.x * 2 + self.core, self.y)

    def line_peer(self, j):
        return ((j // 2) * 8 + self.x * 2 + lax.rem(j, 2), self.y)


class Exchange:
    def __init__(self, sems, row, members, me, peer, src, slots):
        self.send, self.recv = sems
        self.row, self.members, self.me, self.peer = row, members, me, peer
        self.src, self.slots = src, slots

    def copy(self, src, dst, k):
        return pltpu.make_async_remote_copy(
            src,
            dst,
            self.send.at[self.row],
            self.recv.at[self.row],
            device_id=self.peer(lax.rem(self.me + k, self.members)),
            device_id_type=MESH,
        )

    def start(self):
        for k in range(1, self.members):
            src = self.src(lax.rem(self.me + k, self.members))
            self.copy(src, self.slots.at[self.me], k).start()

    def wait(self):
        others = self.slots.at[pl.ds(0, self.members - 1)]
        copy = self.copy(others, others, 1)
        copy.wait_send()
        copy.wait_recv()


def add_slots(ref):
    return jnp.sum(ref[...].astype(F32), axis=0).astype(BF)


class FiveStep:
    def __init__(self, places, sems, row, data, pair, half, got, line, full):
        core, plane = places.core, places.plane
        self.places, self.data, self.pair, self.half = places, data, pair, half
        self.got, self.line, self.full = got, line, full
        self.stages = [
            Exchange(sems, row, 2, core, places.core_peer,
                     lambda j: data.at[j], pair),
            Exchange(sems, row + 1, GROUP, plane, places.plane_peer,
                     lambda j: half.at[j], got),
            Exchange(sems, row + 2, 8, places.z, places.column_peer,
                     lambda j: line.at[places.z], line),
            Exchange(sems, row + 3, GROUP, plane, places.plane_peer,
                     lambda j: full.at[core, plane], full.at[core]),
            Exchange(sems, row + 4, 2, core, places.core_peer,
                     lambda j: full.at[core], full),
        ]

    def begin(self):
        self.stages[0].start()

    def advance(self, stage):
        places = self.places
        core, plane = places.core, places.plane
        self.stages[stage].wait()
        if stage == 0:
            self.half[...] = (
                self.data[core].astype(F32) + self.pair[1 - core].astype(F32)
            ).astype(BF)
            self.got[plane] = self.half[plane]
        if stage == 1:
            self.line[places.z] = add_slots(self.got)
        if stage == 2:
            self.full[core, plane] = add_slots(self.line)
        if stage < 4:
            self.stages[stage + 1].start()


class ThreeStep:
    def __init__(self, places, sems, row, data, got, line, full):
        plane = places.plane
        self.places, self.data, self.got = places, data, got
        self.line, self.full = line, full
        self.stages = [
            Exchange(sems, row, GROUP, plane, places.plane_peer,
                     lambda j: data.at[j], got),
            Exchange(sems, row + 1, GROUP, places.line, places.line_peer,
                     lambda j: line.at[places.line], line),
            Exchange(sems, row + 2, GROUP, plane, places.plane_peer,
                     lambda j: full.at[plane], full),
        ]

    def begin(self):
        plane = self.places.plane
        self.stages[0].start()
        self.got[plane] = self.data[plane]

    def advance(self, stage):
        places = self.places
        self.stages[stage].wait()
        if stage == 0:
            self.line[places.line] = add_slots(self.got)
        if stage == 1:
            self.full[places.plane] = add_slots(self.line)
        if stage < 2:
            self.stages[stage + 1].start()


def backward_kernel(
    counts_ref, parent_ref, feats_ref, gain_ref, w_qkv_ref, w_out_ref, w_down_ref, w_up_ref,
    cot_ref, att_ref, scale_ref, proj_hbm, raised_hbm,
    result_ref, d_feats_ref, early_ref, first_ref, second_ref, third_ref,
    proj_ref, raised_s, hidden_s, sum_s,
    d_hidden_s, normed_s, across_s, d_att_s, d_proj_s, values_s, cots_s, member_s, back_s,
    send_up, recv_up, send_down, recv_down,
    e_data, e_pair, e_half, e_got, e_line, e_full,
    f_data, f_pair, f_half, f_got, f_line, f_full,
    s_data, s_pair, s_half, s_got, s_line, s_full,
    t_data, t_got, t_line, t_full,
    near_send, near_recv, far_send, far_recv, load_sem,
):
    step = pl.program_id(0)
    live = counts_ref[0]
    places = Places()
    sems = (far_send, far_recv)
    early = FiveStep(places, sems, EARLY_ROW, e_data, e_pair, e_half, e_got, e_line, e_full)
    first = FiveStep(places, sems, FIRST_ROW, f_data, f_pair, f_half, f_got, f_line, f_full)
    second = FiveStep(places, sems, SECOND_ROW, s_data, s_pair, s_half, s_got, s_line, s_full)
    third = ThreeStep(places, sems, THIRD_ROW, t_data, t_got, t_line, t_full)
    chunks = {"early": early, "first": first, "second": second, "third": third}
    load_proj = pltpu.make_async_copy(proj_hbm, proj_ref, load_sem.at[2])

    def load_raised(at):
        slot = lax.rem(at, 2)
        return pltpu.make_async_copy(
            raised_hbm.at[pl.ds(at * PAIR, PAIR)], raised_s.at[slot], load_sem.at[slot]
        )

    @pl.when(step == 0)
    def _():
        after, before = neighbour(1), neighbour(-1)
        barrier = pltpu.get_barrier_semaphore()
        for other in (after, before):
            pl.semaphore_signal(barrier, inc=1, device_id=other, device_id_type=MESH)
        for k in range(1, GROUP):
            for other in (
                places.plane_peer(lax.rem(places.plane + k, GROUP)),
                places.line_peer(lax.rem(places.line + k, GROUP)),
            ):
                pl.semaphore_signal(barrier, inc=1, device_id=other, device_id_type=MESH)
        load_proj.start()
        load_raised(0).start()

        attended = att_ref[...].T
        hidden = (
            feats_ref[...].astype(F32) + dg(attended, w_out_ref[...], 1, 0)
        ).astype(BF)
        hidden_s[...] = hidden
        local = parent_ref[...] - device_number() * CORE
        member = (local == iota((TABLE, ROWS), 0)) & (iota((TABLE, ROWS), 1) < live)
        member_f = jnp.where(member, 1.0, 0.0)
        counted = jnp.sum(member_f, axis=1, keepdims=True)
        sum_s[:, :C1] = dg(member_f.astype(BF), hidden, 1, 0)
        sum_s[:, C1 : 2 * C1] = dg(member_f.astype(BF), cot_ref[...], 1, 0)
        sum_s[:, 2 * C1 :] = jnp.broadcast_to(counted, (TABLE, HALF))
        for buf, rows in ((send_up, slice(CORE, TABLE)), (send_down, slice(0, SPILL))):
            buf[:, : 2 * C1] = sum_s[rows, : 2 * C1].astype(BF)
            count = sum_s[rows, 2 * C1 :]
            high = count.astype(BF)
            low = (count - high.astype(F32)).astype(BF)
            buf[:, 2 * C1 :] = jnp.where(iota((SPILL, HALF), 1) < HALF // 2, high, low)
        pl.semaphore_wait(barrier, 2 * GROUP)
        up = pltpu.make_async_remote_copy(
            send_up, recv_up, near_send.at[0], near_recv.at[0],
            device_id=after, device_id_type=MESH,
        )
        down = pltpu.make_async_remote_copy(
            send_down, recv_down, near_send.at[1], near_recv.at[1],
            device_id=before, device_id_type=MESH,
        )
        up.start()
        down.start()

        xhat, _ = norm_parts(feats_ref[...].astype(F32))
        normed = (xhat * gain_ref[...]).astype(BF)
        normed_s[...] = normed
        across_s[...] = normed.T
        values = dg(normed, w_qkv_ref[:, 2 * C1 :], 1, 0).astype(BF)
        ones = jnp.where(iota((ROWS, HALF), 1) < 2, 1.0, 0.0).astype(BF)
        for half in range(2):
            values_s[half, :, :HALF] = values[:, half * HALF : (half + 1) * HALF]
            values_s[half, :, HALF:] = ones
        for one in range(PAIR):
            cots_s[one] = jnp.zeros((C1, ROWS), BF)
        column = jnp.broadcast_to(local.astype(F32), (HALF, ROWS)).T[:, :1].astype(jnp.int32)
        member = (column == iota((ROWS, TABLE), 1)) & (iota((ROWS, TABLE), 0) < live)
        member_s[...] = jnp.where(member, 1.0, 0.0).astype(BF)

        up.wait()
        down.wait()
        sums = []
        for buf, rows in ((recv_up, slice(0, SPILL)), (recv_down, slice(CORE, TABLE))):
            got = buf[...].astype(F32)
            count_in = (
                got[:, 2 * C1 : 2 * C1 + 1]
                + got[:, 2 * C1 + HALF // 2 : 2 * C1 + HALF // 2 + 1]
            )
            sums.append(
                (
                    sum_s[rows, :C1] + got[:, :C1],
                    sum_s[rows, C1 : 2 * C1] + got[:, C1 : 2 * C1],
                    sum_s[rows, 2 * C1 : 2 * C1 + 1] + count_in,
                )
            )
        middle = slice(SPILL, CORE)
        sums.insert(
            1,
            (
                sum_s[middle, :C1],
                sum_s[middle, C1 : 2 * C1],
                sum_s[middle, 2 * C1 : 2 * C1 + 1],
            ),
        )
        own_sum, own_cot, counted = [
            jnp.concatenate([piece[n] for piece in sums], axis=0) for n in range(3)
        ]
        inverse = 1.0 / jnp.maximum(counted, 1.0)
        pooled = (own_sum * inverse).astype(BF)
        pre = dg(pooled, w_down_ref[...], 1, 0)
        value, slope = gelu_and_slope(pre)
        activ = value.astype(BF)
        back_s[...] = dg(activ, w_up_ref[...], 1, 0).astype(BF)
        d_back = own_cot.astype(BF)
        d_pre = (dg(d_back, w_up_ref[...], 1, 1) * slope).astype(BF)
        share = dg(d_pre, w_down_ref[...], 1, 1) * inverse
        share_high = share.astype(BF)
        share_low = (share - share_high.astype(F32)).astype(BF)
        grad_up = dg(activ[:CORE], d_back[:CORE], 0, 0).astype(BF)
        e_data[:, :, :, :C1] = grad_up.reshape(2, GROUP, 16, C1)
        grad_down = dg(pooled[:CORE], d_pre[:CORE], 0, 0).astype(BF).reshape(GROUP, 16, C2)
        for core in range(2):
            e_data[core, :, :, C1 : 2 * C1] = grad_down[:, :, core * C1 : (core + 1) * C1]
        member_b = member_s[...]
        d_hidden = (
            cot_ref[...].astype(F32)
            + dg(member_b, share_high, 1, 0)
            + dg(member_b, share_low, 1, 0)
        )
        d_hidden_s[...] = d_hidden
        d_hidden_b = d_hidden.astype(BF)
        grad_out = dg(att_ref[...], d_hidden_b, 1, 0).astype(BF).reshape(GROUP, 16, C1)
        for core in range(2):
            e_data[core, :, :, 2 * C1 :] = grad_out[:, :, core * HALF : (core + 1) * HALF]
        early.begin()
        d_att_s[...] = dg(w_out_ref[...], d_hidden_b, 1, 1).astype(BF)
        load_proj.wait()

    @pl.when(step < STEPS - 1)
    def _():
        load_raised(step + 1).start()

    load_raised(step).wait()

    def grad_columns(head, heads):
        rows = [
            d_proj_s[part * C1 + head * HD : part * C1 + (head + heads) * HD, :]
            for part in range(3)
        ]
        return dg(across_s[...], jnp.concatenate(rows, axis=0), 1, 1).astype(BF)

    def fill_halves(data, head, heads):
        grads = grad_columns(head, heads)
        width = 3 * heads * HD // 2
        for core in range(2):
            data[core] = grads[:, core * width : (core + 1) * width].reshape(GROUP, 16, width)

    def serve(name, stage):
        if stage >= 0:
            chunks[name].advance(stage)
            return
        if name == "first":
            fill_halves(f_data, 0, FIRST_HEADS)
        else:
            fill_halves(s_data, FIRST_HEADS, SECOND_HEADS)
        chunks[name].begin()

    half = step // (STEPS // 2)
    quarter = jnp.asarray(HD ** (-0.5), BF)
    for one in range(PAIR):
        for turn, name, stage in SERVICES:
            if turn % PAIR == one:
                @pl.when(step == turn // PAIR)
                def _(name=name, stage=stage):
                    serve(name, stage)

        head = step * PAIR + one
        start = pl.multiple_of(head * HD, HD)
        place = pl.multiple_of(lax.rem(head, HEADS // 2) * HD, HD)
        cot = (d_att_s[pl.ds(start, HD), :].astype(F32) * scale_ref[one, :1, :]).astype(BF)
        inner = -jnp.sum(
            cot.astype(F32) * att_ref[pl.ds(start, HD), :].astype(F32), axis=0, keepdims=True
        )
        high = inner.astype(BF).astype(F32)
        rows = iota((HD, ROWS), 0)
        cots_s[one, :HALF, :] = jnp.zeros((HALF, ROWS), BF)
        cots_s[one, pl.ds(place, HD), :] = cot
        cots_s[one, HALF : HALF + HD, :] = jnp.where(
            rows == 0, high, jnp.where(rows == 1, inner - high, 0.0)
        ).astype(BF)
        raised = raised_s[lax.rem(step, 2), one]
        d_scores = raised * dg(values_s[half], cots_s[one], 1, 0).astype(BF)
        d_proj_s[pl.ds(start, HD), :] = dg(
            proj_ref[pl.ds(C1 + start, HD), :] * quarter, d_scores, 1, 0
        ).astype(BF)
        d_proj_s[pl.ds(2 * C1 + start, HD), :] = dg(cot, raised, 1, 1).astype(BF)
        d_proj_s[pl.ds(C1 + start, HD), :] = dg(
            proj_ref[pl.ds(start, HD), :] * quarter, d_scores, 1, 1
        ).astype(BF)

    @pl.when(step == STEPS - 1)
    def _():
        grads = grad_columns(FIRST_HEADS + SECOND_HEADS, THIRD_HEADS)
        t_data[...] = grads.reshape(GROUP, 16, THIRD_W)
        third.begin()
        early.advance(4)
        first.advance(2)
        d_normed = dg(w_qkv_ref[...], d_proj_s[...], 1, 0).T
        second.advance(1)
        xhat, inverse = norm_parts(feats_ref[...].astype(F32))
        grown = d_normed * gain_ref[...]
        along = jnp.mean(grown * xhat, axis=-1, keepdims=True)
        d_wide = inverse * (grown - jnp.mean(grown, axis=-1, keepdims=True) - xhat * along)
        d_feats_ref[...] = (d_hidden_s[...] + d_wide).astype(BF)
        third.advance(0)
        first.advance(3)
        result_ref[...] = (
            hidden_s[...].astype(F32) + dg(member_s[...], back_s[...], 1, 0)
        ).astype(BF)
        early_ref[...] = e_full[...]
        second.advance(2)
        third.advance(1)
        first.advance(4)
        first_ref[...] = f_full[...]
        second.advance(3)
        second.advance(4)
        second_ref[...] = s_full[...]
        third.advance(2)
        third_ref[...] = t_full[...]


def backward_call(
    counts, parent, feats, gain, w_qkv, w_out, w_down, w_up, cotangent,
    att, scale, proj, raised,
):
    out = jax.ShapeDtypeStruct
    vmem = pltpu.VMEM
    early, first, second, third = (
        (2, GROUP, 16, EARLY_W),
        (2, GROUP, 16, FIRST_W),
        (2, GROUP, 16, SECOND_W),
        (GROUP, 16, THIRD_W),
    )

    def five(shape):
        return [
            vmem(shape, BF), vmem(shape, BF), vmem(shape[1:], BF), vmem(shape[1:], BF),
            vmem((8,) + shape[2:], BF), vmem(shape, BF),
        ]

    return pl.pallas_call(
        backward_kernel,
        grid=(STEPS,),
        in_specs=[
            pl.BlockSpec(memory_space=pltpu.SMEM),
            whole((1, ROWS)),
            whole((ROWS, C1)),
            whole((1, C1)),
            whole((C1, 3 * C1)),
            whole((C1, C1)),
            whole((C1, C2)),
            whole((C2, C1)),
            whole((ROWS, C1)),
            whole((C1, ROWS)),
            per_pair(8),
            pl.BlockSpec(memory_space=pl.ANY),
            pl.BlockSpec(memory_space=pl.ANY),
        ],
        out_specs=[
            whole((ROWS, C1)),
            whole((ROWS, C1)),
            whole(early),
            whole(first),
            whole(second),
            whole(third),
        ],
        out_shape=[
            out((ROWS, C1), BF),
            out((ROWS, C1), BF),
            out(early, BF),
            out(first, BF),
            out(second, BF),
            out(third, BF),
        ],
        scratch_shapes=[
            vmem((3 * C1, ROWS), BF),
            vmem((2, PAIR, ROWS, ROWS), BF),
            vmem((ROWS, C1), BF),
            vmem((TABLE, UP_W), F32),
            vmem((ROWS, C1), F32),
            vmem((ROWS, C1), BF),
            vmem((C1, ROWS), BF),
            vmem((C1, ROWS), BF),
            vmem((3 * C1, ROWS), BF),
            vmem((2, ROWS, C1), BF),
            vmem((PAIR, C1, ROWS), BF),
            vmem((ROWS, TABLE), BF),
            vmem((TABLE, C1), BF),
            vmem((SPILL, UP_W), BF),
            vmem((SPILL, UP_W), BF),
            vmem((SPILL, UP_W), BF),
            vmem((SPILL, UP_W), BF),
        ]
        + five(early)
        + five(first)
        + five(second)
        + [vmem(third, BF)] * 4
        + [
            pltpu.SemaphoreType.DMA((2,)),
            pltpu.SemaphoreType.DMA((2,)),
            pltpu.SemaphoreType.DMA((18,)),
            pltpu.SemaphoreType.DMA((18,)),
            pltpu.SemaphoreType.DMA((3,)),
        ],
        compiler_params=pltpu.CompilerParams(
            collective_id=0, has_side_effects=True, vmem_limit_bytes=58 * 2**20
        ),
        name="backward",
    )(
        counts, parent, feats, gain, w_qkv, w_out, w_down, w_up, cotangent,
        att, scale, proj, raised,
    )


def finish_kernel(
    result_ref, d_feats_ref, early_ref, first_ref, second_ref, third_ref,
    result_out, d_feats_out, qkv_out, out_out, down_out, up_out,
):
    result_out[...] = result_ref[...]
    d_feats_out[...] = d_feats_ref[...]
    for core in range(2):
        piece = early_ref[core]
        up_out[core * C1 : (core + 1) * C1, :] = piece[:, :, :C1].reshape(C1, C1).astype(F32)
        down_out[:, core * C1 : (core + 1) * C1] = (
            piece[:, :, C1 : 2 * C1].reshape(C1, C1).astype(F32)
        )
        out_out[:, core * HALF : (core + 1) * HALF] = (
            piece[:, :, 2 * C1 :].reshape(C1, HALF).astype(F32)
        )
    low, high = [
        jnp.concatenate([ref[core].reshape(C1, width).astype(F32) for core in range(2)], axis=1)
        for ref, width in ((first_ref, FIRST_W), (second_ref, SECOND_W))
    ]
    last = third_ref[...].reshape(C1, THIRD_W).astype(F32)
    for part in range(3):
        qkv_out[:, part * C1 : (part + 1) * C1] = jnp.concatenate(
            [
                piece[:, part * heads * HD : (part + 1) * heads * HD]
                for piece, heads in (
                    (low, FIRST_HEADS), (high, SECOND_HEADS), (last, THIRD_HEADS)
                )
            ],
            axis=1,
        )


def finish_call(*parts):
    shapes = [
        ((ROWS, C1), BF), ((ROWS, C1), BF), ((C1, 3 * C1), F32), ((C1, C1), F32),
        ((C1, C2), F32), ((C2, C1), F32),
    ]
    return pl.pallas_call(
        finish_kernel,
        grid=(1,),
        in_specs=[whole(part.shape) for part in parts],
        out_specs=[whole(shape) for shape, _ in shapes],
        out_shape=[jax.ShapeDtypeStruct(shape, kind) for shape, kind in shapes],
        compiler_params=pltpu.CompilerParams(vmem_limit_bytes=60 * 2**20),
        name="finish",
    )(*parts)


def per_device(feats, counts, parent, ln_gain, w_qkv, w_out, w_down, w_up, cotangent):
    parent_row = parent.reshape(1, ROWS)
    gain = ln_gain.reshape(1, C1)
    raised, proj, scale, att = forward_call(counts, feats, gain, w_qkv)
    parts = backward_call(
        counts, parent_row, feats, gain, w_qkv, w_out, w_down, w_up, cotangent,
        att, scale, proj, raised,
    )
    return tuple(finish_call(*parts))


def solution(mesh):
    rows = P(("pts", "grp"), None)
    line = P(("pts", "grp"))
    return jax.shard_map(
        per_device,
        mesh=mesh,
        in_specs=(rows, line, line, P(), P(), P(), P(), P(), rows),
        out_specs=(rows, rows, P(), P(), P(), P()),
        check_vma=False,
    )
```

```python
import jax
import jax.numpy as jnp
from jax import lax
from jax.experimental import pallas as pl
from jax.experimental.pallas import tpu as pltpu
from jax.sharding import PartitionSpec as P

HD = 16
HEADS = 16
ROWS = 1024
C1 = 256
C2 = 512
CORE = 256
SPILL = 64
TABLE = CORE + SPILL
PAIR = 2
STEPS = HEADS // PAIR
HALF = 128
BAND = 64
BANDS = C1 // BAND
SAFE_SCORE = 60.0
MESH = pl.DeviceIdType.MESH
BF = jnp.bfloat16
F32 = jnp.float32


def dg(left, right, left_dim, right_dim):
    return lax.dot_general(
        left,
        right,
        (((left_dim,), (right_dim,)), ((), ())),
        preferred_element_type=F32,
    )


def iota(shape, dim):
    return lax.broadcasted_iota(jnp.int32, shape, dim)


def norm_parts(wide):
    center = wide - jnp.mean(wide, axis=-1, keepdims=True)
    spread = jnp.mean(center * center, axis=-1, keepdims=True)
    inverse = lax.rsqrt(spread + 1e-05)
    return center * inverse, inverse


def device_number():
    return lax.axis_index("pts") * lax.axis_size("grp") + lax.axis_index("grp")


def whole(shape):
    return pl.BlockSpec(shape, lambda i, n=len(shape): (0,) * n)


def per_pair(rows):
    return pl.BlockSpec((PAIR, rows, ROWS), lambda i: (i, 0, 0))


def forward_kernel(
    counts_ref, feats_ref, gain_ref, w_qkv_ref,
    raised_hbm, proj_hbm, scale_ref, att_ref,
    proj_ref, raised_s, keys_s, query_s, mixed_s, safe_s, store_sem, proj_sem,
):
    step = pl.program_id(0)
    live = counts_ref[0]
    slot = lax.rem(step, 2)
    store_proj = pltpu.make_async_copy(proj_ref, proj_hbm, proj_sem.at[0])

    def store(at, one):
        place = lax.rem(at, 2)
        return pltpu.make_async_copy(
            raised_s.at[place, one], raised_hbm.at[at * PAIR + one], store_sem.at[place, one]
        )

    @pl.when(step == 0)
    def _():
        xhat, _ = norm_parts(feats_ref[...].astype(F32))
        normed = (xhat * gain_ref[...]).astype(BF)
        proj = dg(w_qkv_ref[...], normed, 0, 1).astype(BF)
        proj_ref[...] = proj
        store_proj.start()
        keys = dg(normed, w_qkv_ref[:, C1 : 2 * C1], 1, 0).astype(BF)
        dead = (iota((ROWS, BAND), 0) >= live) & (iota((ROWS, BAND), 1) == 0)
        bias = jnp.where(dead, -1e30, 0.0).astype(BF)
        for band in range(BANDS):
            keys_s[band] = jnp.concatenate(
                [keys[:, band * BAND : (band + 1) * BAND], bias], axis=1
            )
        ones = jnp.where(iota((BAND, ROWS), 0) == 0, 1.0, 0.0).astype(BF)
        for one in range(PAIR):
            query_s[one, BAND:, :] = ones
        wide = proj[: 2 * C1, :].astype(F32)
        squares = jnp.sum((wide * wide).reshape(2, HEADS, HD, ROWS), axis=2)
        bound = jnp.max(squares[0]) * jnp.max(squares[1]) / HD
        safe_s[0] = (bound <= SAFE_SCORE * SAFE_SCORE).astype(jnp.int32)

    band = step // (STEPS // BANDS)
    for one in range(PAIR):
        head = step * PAIR + one
        start = pl.multiple_of(head * HD, HD)
        place = pl.multiple_of(lax.rem(head, BAND // HD) * HD, HD)
        query_s[one, :BAND, :] = jnp.zeros((BAND, ROWS), BF)
        query_s[one, pl.ds(place, HD), :] = proj_ref[pl.ds(start, HD), :] * jnp.asarray(
            HD ** (-0.5), BF
        )

    @pl.when(step >= 2)
    def _():
        for one in range(PAIR):
            store(step - 2, one).wait()

    def attend(one, shifted):
        scores = dg(keys_s[band], query_s[one], 1, 0)
        if shifted:
            scores = scores - jnp.max(scores, axis=0, keepdims=True)
        raised = jnp.exp(scores)
        scale = 1.0 / jnp.sum(raised, axis=0, keepdims=True)
        raised_b = raised.astype(BF)
        raised_s[slot, one] = raised_b
        start = pl.multiple_of((step * PAIR + one) * HD, HD)
        mixed_s[one] = dg(proj_ref[pl.ds(2 * C1 + start, HD), :], raised_b, 1, 0) * scale
        scale_ref[one] = jnp.broadcast_to(scale, (8, ROWS))
        store(step, one).start()

    @pl.when(safe_s[0] == 1)
    def _():
        for one in range(PAIR):
            attend(one, False)

    @pl.when(safe_s[0] != 1)
    def _():
        for one in range(PAIR):
            attend(one, True)

    for one in range(PAIR):
        start = pl.multiple_of((step * PAIR + one) * HD, HD)
        att_ref[pl.ds(start, HD), :] = mixed_s[one].astype(BF)

    @pl.when(step == STEPS - 1)
    def _():
        store_proj.wait()
        for one in range(PAIR):
            store(step - 1, one).wait()
            store(step, one).wait()


def forward_call(counts, feats, gain, w_qkv):
    out = jax.ShapeDtypeStruct
    return pl.pallas_call(
        forward_kernel,
        grid=(STEPS,),
        in_specs=[
            pl.BlockSpec(memory_space=pltpu.SMEM),
            whole((ROWS, C1)),
            whole((1, C1)),
            whole((C1, 3 * C1)),
        ],
        out_specs=[
            pl.BlockSpec(memory_space=pl.ANY),
            pl.BlockSpec(memory_space=pl.ANY),
            per_pair(8),
            whole((C1, ROWS)),
        ],
        out_shape=[
            out((HEADS, ROWS, ROWS), BF),
            out((3 * C1, ROWS), BF),
            out((HEADS, 8, ROWS), F32),
            out((C1, ROWS), BF),
        ],
        scratch_shapes=[
            pltpu.VMEM((3 * C1, ROWS), BF),
            pltpu.VMEM((2, PAIR, ROWS, ROWS), BF),
            pltpu.VMEM((BANDS, ROWS, HALF), BF),
            pltpu.VMEM((PAIR, HALF, ROWS), BF),
            pltpu.VMEM((PAIR, HD, ROWS), F32),
            pltpu.SMEM((1,), jnp.int32),
            pltpu.SemaphoreType.DMA((2, PAIR)),
            pltpu.SemaphoreType.DMA((1,)),
        ],
        compiler_params=pltpu.CompilerParams(vmem_limit_bytes=56 * 2**20),
        name="forward",
    )(counts, feats, gain, w_qkv)


def gelu_and_slope(pre):
    root = 0.7978845608028654
    square = pre * pre
    tanh = jnp.tanh(root * (pre + 0.044715 * (square * pre)))
    value = pre * (0.5 * (1.0 + tanh))
    slope = 0.5 * (1.0 + tanh) + 0.5 * pre * (1.0 - tanh * tanh) * root * (
        1.0 + 3 * 0.044715 * square
    )
    return value, slope


def neighbour(distance):
    devices = lax.axis_size("pts") * lax.axis_size("grp")
    other = lax.rem(device_number() + distance + devices, devices)
    return (other // lax.axis_size("grp"), lax.rem(other, lax.axis_size("grp")))


GROUP = 16
UP_W = 2 * C1 + HALF
EARLY_HEADS, LATE_HEADS, LAST_HEADS = 4, 10, 2
GRADS_W = 2 * C1 + HALF
EARLY_W = GRADS_W + EARLY_HEADS * 24
LATE_W, LAST_W = LATE_HEADS * 24, LAST_HEADS * 48
EARLY_ROW, LATE_ROW, LAST_ROW = 0, 5, 10
SERVICES = (
    (4, "early", -1), (5, "early", 0), (9, "early", 1), (13, "early", 2),
    (14, "late", -1), (15, "late", 0),
)


class Places:
    def __init__(self):
        pts, self.y = lax.axis_index("pts"), lax.axis_index("grp")
        self.core = lax.rem(pts, 2)
        self.x = lax.rem(pts // 2, 4)
        self.z = pts // 8
        self.plane = self.x * 4 + self.y
        self.line = self.z * 2 + self.core

    def core_peer(self, j):
        return (self.z * 8 + self.x * 2 + j, self.y)

    def plane_peer(self, j):
        return (self.z * 8 + (j // 4) * 2 + self.core, lax.rem(j, 4))

    def column_peer(self, j):
        return (j * 8 + self.x * 2 + self.core, self.y)

    def line_peer(self, j):
        return ((j // 2) * 8 + self.x * 2 + lax.rem(j, 2), self.y)


class Exchange:
    def __init__(self, sems, row, members, me, peer, src, slots):
        self.send, self.recv = sems
        self.row, self.members, self.me, self.peer = row, members, me, peer
        self.src, self.slots = src, slots

    def copy(self, src, dst, k):
        return pltpu.make_async_remote_copy(
            src,
            dst,
            self.send.at[self.row],
            self.recv.at[self.row],
            device_id=self.peer(lax.rem(self.me + k, self.members)),
            device_id_type=MESH,
        )

    def start(self):
        for k in range(1, self.members):
            src = self.src(lax.rem(self.me + k, self.members))
            self.copy(src, self.slots.at[self.me], k).start()

    def wait(self):
        others = self.slots.at[pl.ds(0, self.members - 1)]
        copy = self.copy(others, others, 1)
        copy.wait_send()
        copy.wait_recv()


def add_slots(ref):
    return jnp.sum(ref[...].astype(F32), axis=0).astype(BF)


class FiveStep:
    def __init__(self, places, sems, row, data, pair, half, got, line, full):
        core, plane = places.core, places.plane
        self.places, self.data, self.pair, self.half = places, data, pair, half
        self.got, self.line, self.full = got, line, full
        self.stages = [
            Exchange(sems, row, 2, core, places.core_peer,
                     lambda j: data.at[j], pair),
            Exchange(sems, row + 1, GROUP, plane, places.plane_peer,
                     lambda j: half.at[j], got),
            Exchange(sems, row + 2, 8, places.z, places.column_peer,
                     lambda j: line.at[places.z], line),
            Exchange(sems, row + 3, GROUP, plane, places.plane_peer,
                     lambda j: full.at[core, plane], full.at[core]),
            Exchange(sems, row + 4, 2, core, places.core_peer,
                     lambda j: full.at[core], full),
        ]

    def begin(self):
        self.stages[0].start()

    def advance(self, stage):
        places = self.places
        core, plane = places.core, places.plane
        self.stages[stage].wait()
        if stage == 0:
            self.half[...] = (
                self.data[core].astype(F32) + self.pair[1 - core].astype(F32)
            ).astype(BF)
            self.got[plane] = self.half[plane]
        if stage == 1:
            self.line[places.z] = add_slots(self.got)
        if stage == 2:
            self.full[core, plane] = add_slots(self.line)
        if stage < 4:
            self.stages[stage + 1].start()


class ThreeStep:
    def __init__(self, places, sems, row, data, got, line, full):
        plane = places.plane
        self.places, self.data, self.got = places, data, got
        self.line, self.full = line, full
        self.stages = [
            Exchange(sems, row, GROUP, plane, places.plane_peer,
                     lambda j: data.at[j], got),
            Exchange(sems, row + 1, GROUP, places.line, places.line_peer,
                     lambda j: line.at[places.line], line),
            Exchange(sems, row + 2, GROUP, plane, places.plane_peer,
                     lambda j: full.at[plane], full),
        ]

    def begin(self):
        plane = self.places.plane
        self.stages[0].start()
        self.got[plane] = self.data[plane]

    def advance(self, stage):
        places = self.places
        self.stages[stage].wait()
        if stage == 0:
            self.line[places.line] = add_slots(self.got)
        if stage == 1:
            self.full[places.plane] = add_slots(self.line)
        if stage < 2:
            self.stages[stage + 1].start()


def backward_kernel(
    counts_ref, parent_ref, gain_ref,
    att_hbm, feats_hbm, w_out_hbm, cot_hbm, w_qkv_hbm, w_down_hbm, w_up_hbm, proj_hbm, scale_hbm,
    raised_hbm,
    result_hbm, d_feats_hbm, early_hbm, late_hbm, last_hbm,
    att_ref, feats_ref, w_out_ref, cot_ref, w_qkv_ref, w_down_ref, w_up_ref, proj_ref, scale_ref,
    result_s, d_feats_s, raised_s, hidden_s, sum_s,
    d_hidden_s, normed_s, across_s, d_att_s, d_proj_s, values_s, cots_s, member_s, back_s,
    send_up, recv_up, send_down, recv_down,
    e_data, e_pair, e_half, e_got, e_line, e_full,
    f_data, f_pair, f_half, f_got, f_line, f_full,
    t_data, t_got, t_line, t_full,
    near_send, near_recv, far_send, far_recv, load_sem, raised_sem, store_sem,
):
    step = pl.program_id(0)
    live = counts_ref[0]
    places = Places()
    sems = (far_send, far_recv)
    early = FiveStep(places, sems, EARLY_ROW, e_data, e_pair, e_half, e_got, e_line, e_full)
    late = FiveStep(places, sems, LATE_ROW, f_data, f_pair, f_half, f_got, f_line, f_full)
    last = ThreeStep(places, sems, LAST_ROW, t_data, t_got, t_line, t_full)
    chunks = {"early": early, "late": late}
    loads = [
        pltpu.make_async_copy(src, dst, load_sem.at[n])
        for n, (src, dst) in enumerate(
            (
                (att_hbm, att_ref), (feats_hbm, feats_ref), (w_out_hbm, w_out_ref),
                (cot_hbm, cot_ref), (w_qkv_hbm, w_qkv_ref), (w_down_hbm, w_down_ref),
                (w_up_hbm, w_up_ref), (proj_hbm, proj_ref), (scale_hbm, scale_ref),
            )
        )
    ]
    stores = [
        pltpu.make_async_copy(src, dst, store_sem.at[n])
        for n, (src, dst) in enumerate(
            (
                (result_s, result_hbm), (d_feats_s, d_feats_hbm), (e_full, early_hbm),
                (f_full, late_hbm), (t_full, last_hbm),
            )
        )
    ]

    def load_raised(at):
        slot = lax.rem(at, 2)
        return pltpu.make_async_copy(
            raised_hbm.at[pl.ds(at * PAIR, PAIR)], raised_s.at[slot], raised_sem.at[slot]
        )

    @pl.when(step == 0)
    def _():
        for load in loads[:7]:
            load.start()
        after, before = neighbour(1), neighbour(-1)
        barrier = pltpu.get_barrier_semaphore()
        for other in (after, before):
            pl.semaphore_signal(barrier, inc=1, device_id=other, device_id_type=MESH)
        for k in range(1, GROUP):
            for other in (
                places.plane_peer(lax.rem(places.plane + k, GROUP)),
                places.line_peer(lax.rem(places.line + k, GROUP)),
            ):
                pl.semaphore_signal(barrier, inc=1, device_id=other, device_id_type=MESH)
        for load in loads[7:]:
            load.start()
        load_raised(0).start()
        for load in loads[:4]:
            load.wait()

        attended = att_ref[...].T
        hidden = (
            feats_ref[...].astype(F32) + dg(attended, w_out_ref[...], 1, 0)
        ).astype(BF)
        hidden_s[...] = hidden
        local = parent_ref[...] - device_number() * CORE
        member = (local == iota((TABLE, ROWS), 0)) & (iota((TABLE, ROWS), 1) < live)
        member_f = jnp.where(member, 1.0, 0.0)
        counted = jnp.sum(member_f, axis=1, keepdims=True)
        sum_s[:, :C1] = dg(member_f.astype(BF), hidden, 1, 0)
        sum_s[:, C1 : 2 * C1] = dg(member_f.astype(BF), cot_ref[...], 1, 0)
        sum_s[:, 2 * C1 :] = jnp.broadcast_to(counted, (TABLE, HALF))
        for buf, rows in ((send_up, slice(CORE, TABLE)), (send_down, slice(0, SPILL))):
            buf[:, : 2 * C1] = sum_s[rows, : 2 * C1].astype(BF)
            count = sum_s[rows, 2 * C1 :]
            high = count.astype(BF)
            low = (count - high.astype(F32)).astype(BF)
            buf[:, 2 * C1 :] = jnp.where(iota((SPILL, HALF), 1) < HALF // 2, high, low)
        pl.semaphore_wait(barrier, 2 * GROUP)
        up = pltpu.make_async_remote_copy(
            send_up, recv_up, near_send.at[0], near_recv.at[0],
            device_id=after, device_id_type=MESH,
        )
        down = pltpu.make_async_remote_copy(
            send_down, recv_down, near_send.at[1], near_recv.at[1],
            device_id=before, device_id_type=MESH,
        )
        up.start()
        down.start()

        for load in loads[4:7]:
            load.wait()
        xhat, _ = norm_parts(feats_ref[...].astype(F32))
        normed = (xhat * gain_ref[...]).astype(BF)
        normed_s[...] = normed
        across_s[...] = normed.T
        values = dg(normed, w_qkv_ref[:, 2 * C1 :], 1, 0).astype(BF)
        ones = jnp.where(iota((ROWS, BAND), 1) < 2, 1.0, 0.0).astype(BF)
        for band in range(BANDS):
            values_s[band] = jnp.concatenate(
                [values[:, band * BAND : (band + 1) * BAND], ones], axis=1
            )
        for one in range(PAIR):
            cots_s[one] = jnp.zeros((HALF, ROWS), BF)
        column = jnp.broadcast_to(local.astype(F32), (HALF, ROWS)).T[:, :1].astype(jnp.int32)
        member = (column == iota((ROWS, TABLE), 1)) & (iota((ROWS, TABLE), 0) < live)
        member_s[...] = jnp.where(member, 1.0, 0.0).astype(BF)

        up.wait()
        down.wait()
        sums = []
        for buf, rows in ((recv_up, slice(0, SPILL)), (recv_down, slice(CORE, TABLE))):
            got = buf[...].astype(F32)
            count_in = (
                got[:, 2 * C1 : 2 * C1 + 1]
                + got[:, 2 * C1 + HALF // 2 : 2 * C1 + HALF // 2 + 1]
            )
            sums.append(
                (
                    sum_s[rows, :C1] + got[:, :C1],
                    sum_s[rows, C1 : 2 * C1] + got[:, C1 : 2 * C1],
                    sum_s[rows, 2 * C1 : 2 * C1 + 1] + count_in,
                )
            )
        middle = slice(SPILL, CORE)
        sums.insert(
            1,
            (
                sum_s[middle, :C1],
                sum_s[middle, C1 : 2 * C1],
                sum_s[middle, 2 * C1 : 2 * C1 + 1],
            ),
        )
        own_sum, own_cot, counted = [
            jnp.concatenate([piece[n] for piece in sums], axis=0) for n in range(3)
        ]
        inverse = 1.0 / jnp.maximum(counted, 1.0)
        pooled = (own_sum * inverse).astype(BF)
        pre = dg(pooled, w_down_ref[...], 1, 0)
        value, slope = gelu_and_slope(pre)
        activ = value.astype(BF)
        back_s[...] = dg(activ, w_up_ref[...], 1, 0).astype(BF)
        d_back = own_cot.astype(BF)
        d_pre = (dg(d_back, w_up_ref[...], 1, 1) * slope).astype(BF)
        share = dg(d_pre, w_down_ref[...], 1, 1) * inverse
        share_high = share.astype(BF)
        share_low = (share - share_high.astype(F32)).astype(BF)
        grad_up = dg(activ[:CORE], d_back[:CORE], 0, 0).astype(BF)
        grad_up = grad_up.reshape(GROUP, 2, 16, C1)
        grad_down = dg(pooled[:CORE], d_pre[:CORE], 0, 0).astype(BF).reshape(GROUP, 16, C2)
        for core in range(2):
            e_data[core, :, :, :C1] = grad_up[:, core]
            e_data[core, :, :, C1 : 2 * C1] = grad_down[:, :, core * C1 : (core + 1) * C1]
        member_b = member_s[...]
        d_hidden = (
            cot_ref[...].astype(F32)
            + dg(member_b, share_high, 1, 0)
            + dg(member_b, share_low, 1, 0)
        )
        d_hidden_s[...] = d_hidden
        d_hidden_b = d_hidden.astype(BF)
        grad_out = dg(att_ref[...], d_hidden_b, 1, 0).astype(BF).reshape(GROUP, 16, C1)
        for core in range(2):
            e_data[core, :, :, 2 * C1 : GRADS_W] = grad_out[:, :, core * HALF : (core + 1) * HALF]
        d_att_s[...] = dg(w_out_ref[...], d_hidden_b, 1, 1).astype(BF)
        for load in loads[7:]:
            load.wait()

    @pl.when(step < STEPS - 1)
    def _():
        load_raised(step + 1).start()

    load_raised(step).wait()

    def grad_columns(head, heads):
        rows = [
            d_proj_s[part * C1 + head * HD : part * C1 + (head + heads) * HD, :]
            for part in range(3)
        ]
        return dg(across_s[...], jnp.concatenate(rows, axis=0), 1, 1).astype(BF)

    def fill_halves(data, first, head, heads):
        grads = grad_columns(head, heads)
        width = 3 * heads * HD // 2
        for core in range(2):
            data[core, :, :, first : first + width] = grads[
                :, core * width : (core + 1) * width
            ].reshape(GROUP, 16, width)

    def serve(name, stage):
        if stage >= 0:
            chunks[name].advance(stage)
            return
        if name == "early":
            fill_halves(e_data, GRADS_W, 0, EARLY_HEADS)
        else:
            fill_halves(f_data, 0, EARLY_HEADS, LATE_HEADS)
        chunks[name].begin()

    band = step // (STEPS // BANDS)
    quarter = jnp.asarray(HD ** (-0.5), BF)
    for one in range(PAIR):
        for turn, name, stage in SERVICES:
            if turn % PAIR == one:
                @pl.when(step == turn // PAIR)
                def _(name=name, stage=stage):
                    serve(name, stage)

        head = step * PAIR + one
        start = pl.multiple_of(head * HD, HD)
        place = pl.multiple_of(lax.rem(head, BAND // HD) * HD, HD)
        cot = (d_att_s[pl.ds(start, HD), :].astype(F32) * scale_ref[head, :1, :]).astype(BF)
        inner = -jnp.sum(
            cot.astype(F32) * att_ref[pl.ds(start, HD), :].astype(F32), axis=0, keepdims=True
        )
        high = inner.astype(BF).astype(F32)
        rows = iota((HD, ROWS), 0)
        cots_s[one, :BAND, :] = jnp.zeros((BAND, ROWS), BF)
        cots_s[one, pl.ds(place, HD), :] = cot
        cots_s[one, BAND : BAND + HD, :] = jnp.where(
            rows == 0, high, jnp.where(rows == 1, inner - high, 0.0)
        ).astype(BF)
        raised = raised_s[lax.rem(step, 2), one]
        d_scores = raised * dg(values_s[band], cots_s[one], 1, 0).astype(BF)
        d_proj_s[pl.ds(start, HD), :] = dg(
            proj_ref[pl.ds(C1 + start, HD), :] * quarter, d_scores, 1, 0
        ).astype(BF)
        d_proj_s[pl.ds(2 * C1 + start, HD), :] = dg(cot, raised, 1, 1).astype(BF)
        d_proj_s[pl.ds(C1 + start, HD), :] = dg(
            proj_ref[pl.ds(start, HD), :] * quarter, d_scores, 1, 1
        ).astype(BF)

    @pl.when(step == STEPS - 1)
    def _():
        grads = grad_columns(EARLY_HEADS + LATE_HEADS, LAST_HEADS)
        t_data[...] = grads.reshape(GROUP, 16, LAST_W)
        last.begin()
        d_normed = dg(w_qkv_ref[...], d_proj_s[...], 1, 0).T
        early.advance(3)
        late.advance(1)
        xhat, inverse = norm_parts(feats_ref[...].astype(F32))
        grown = d_normed * gain_ref[...]
        along = jnp.mean(grown * xhat, axis=-1, keepdims=True)
        d_wide = inverse * (grown - jnp.mean(grown, axis=-1, keepdims=True) - xhat * along)
        d_feats_s[...] = (d_hidden_s[...] + d_wide).astype(BF)
        stores[1].start()
        last.advance(0)
        early.advance(4)
        stores[2].start()
        result_s[...] = (
            hidden_s[...].astype(F32) + dg(member_s[...], back_s[...], 1, 0)
        ).astype(BF)
        stores[0].start()
        late.advance(2)
        last.advance(1)
        late.advance(3)
        late.advance(4)
        stores[3].start()
        last.advance(2)
        stores[4].start()
        for store in stores:
            store.wait()


def backward_call(counts, parent, gain, att, feats, w_out, cotangent, w_qkv, w_down, w_up,
                  proj, scale, raised):
    out = jax.ShapeDtypeStruct
    vmem = pltpu.VMEM
    anywhere = pl.BlockSpec(memory_space=pl.ANY)
    early, late, last = (
        (2, GROUP, 16, EARLY_W),
        (2, GROUP, 16, LATE_W),
        (GROUP, 16, LAST_W),
    )
    loaded = (att, feats, w_out, cotangent, w_qkv, w_down, w_up, proj, scale)

    def five(shape):
        return [
            vmem(shape, BF), vmem(shape, BF), vmem(shape[1:], BF), vmem(shape[1:], BF),
            vmem((8,) + shape[2:], BF), vmem(shape, BF),
        ]

    return pl.pallas_call(
        backward_kernel,
        grid=(STEPS,),
        in_specs=[
            pl.BlockSpec(memory_space=pltpu.SMEM),
            whole((1, ROWS)),
            whole((1, C1)),
        ]
        + [anywhere] * 10,
        out_specs=[anywhere] * 5,
        out_shape=[
            out((ROWS, C1), BF),
            out((ROWS, C1), BF),
            out(early, BF),
            out(late, BF),
            out(last, BF),
        ],
        scratch_shapes=[vmem(array.shape, array.dtype) for array in loaded]
        + [
            vmem((ROWS, C1), BF),
            vmem((ROWS, C1), BF),
            vmem((2, PAIR, ROWS, ROWS), BF),
            vmem((ROWS, C1), BF),
            vmem((TABLE, UP_W), F32),
            vmem((ROWS, C1), F32),
            vmem((ROWS, C1), BF),
            vmem((C1, ROWS), BF),
            vmem((C1, ROWS), BF),
            vmem((3 * C1, ROWS), BF),
            vmem((BANDS, ROWS, HALF), BF),
            vmem((PAIR, HALF, ROWS), BF),
            vmem((ROWS, TABLE), BF),
            vmem((TABLE, C1), BF),
            vmem((SPILL, UP_W), BF),
            vmem((SPILL, UP_W), BF),
            vmem((SPILL, UP_W), BF),
            vmem((SPILL, UP_W), BF),
        ]
        + five(early)
        + five(late)
        + [vmem(last, BF)] * 4
        + [
            pltpu.SemaphoreType.DMA((2,)),
            pltpu.SemaphoreType.DMA((2,)),
            pltpu.SemaphoreType.DMA((13,)),
            pltpu.SemaphoreType.DMA((13,)),
            pltpu.SemaphoreType.DMA((9,)),
            pltpu.SemaphoreType.DMA((2,)),
            pltpu.SemaphoreType.DMA((5,)),
        ],
        compiler_params=pltpu.CompilerParams(
            collective_id=0, has_side_effects=True, vmem_limit_bytes=58 * 2**20
        ),
        name="backward",
    )(counts, parent, gain, *loaded, raised)


def finish_kernel(
    result_hbm, d_feats_hbm, early_hbm, late_hbm, last_hbm,
    result_out, d_feats_out, qkv_out, out_out, down_out, up_out,
    result_s, d_feats_s, early_ref, late_ref, last_ref, qkv_s, out_s, down_s, up_s, load_sem, pass_sem, store_sem,
):
    loads = [
        pltpu.make_async_copy(src, dst, load_sem.at[n])
        for n, (src, dst) in enumerate(
            (
                (early_hbm, early_ref), (late_hbm, late_ref), (last_hbm, last_ref),
                (result_hbm, result_s), (d_feats_hbm, d_feats_s),
            )
        )
    ]
    passes = [
        pltpu.make_async_copy(result_s, result_out, pass_sem.at[0]),
        pltpu.make_async_copy(d_feats_s, d_feats_out, pass_sem.at[1]),
    ]
    stores = [
        pltpu.make_async_copy(src, dst, store_sem.at[n])
        for n, (src, dst) in enumerate(
            ((qkv_s, qkv_out), (out_s, out_out), (down_s, down_out), (up_s, up_out))
        )
    ]
    for load in loads:
        load.start()
    loads[0].wait()
    for core in range(2):
        up_s[:, core] = early_ref[core, :, :, :C1].astype(F32)
        down_s[:, core * C1 : (core + 1) * C1] = (
            early_ref[core, :, :, C1 : 2 * C1].reshape(C1, C1).astype(F32)
        )
        out_s[:, core * HALF : (core + 1) * HALF] = (
            early_ref[core, :, :, 2 * C1 : GRADS_W].reshape(C1, HALF).astype(F32)
        )
    for store in stores[1:]:
        store.start()
    for load in loads[1:]:
        load.wait()
    for one in passes:
        one.start()
    early, late = [
        jnp.concatenate(
            [ref[core, :, :, first:].astype(F32).reshape(C1, -1) for core in range(2)], axis=1
        )
        for ref, first in ((early_ref, GRADS_W), (late_ref, 0))
    ]
    last = last_ref[...].astype(F32).reshape(C1, LAST_W)
    for part in range(3):
        qkv_s[:, part * C1 : (part + 1) * C1] = jnp.concatenate(
            [
                piece[:, part * heads * HD : (part + 1) * heads * HD]
                for piece, heads in (
                    (early, EARLY_HEADS), (late, LATE_HEADS), (last, LAST_HEADS)
                )
            ],
            axis=1,
        )
    stores[0].start()
    for copy in passes + stores:
        copy.wait()


def finish_call(*parts):
    anywhere = pl.BlockSpec(memory_space=pl.ANY)
    shapes = [
        ((ROWS, C1), BF), ((ROWS, C1), BF), ((C1, 3 * C1), F32), ((C1, C1), F32),
        ((C1, C2), F32), ((GROUP, 2, 16, C1), F32),
    ]
    return pl.pallas_call(
        finish_kernel,
        in_specs=[anywhere] * 5,
        out_specs=[anywhere] * 6,
        out_shape=[jax.ShapeDtypeStruct(shape, kind) for shape, kind in shapes],
        scratch_shapes=[pltpu.VMEM(part.shape, BF) for part in parts]
        + [pltpu.VMEM(shape, F32) for shape, _ in shapes[2:]]
        + [
            pltpu.SemaphoreType.DMA((5,)),
            pltpu.SemaphoreType.DMA((2,)),
            pltpu.SemaphoreType.DMA((4,)),
        ],
        compiler_params=pltpu.CompilerParams(vmem_limit_bytes=60 * 2**20),
        name="finish",
    )(*parts)


def per_device(feats, counts, parent, ln_gain, w_qkv, w_out, w_down, w_up, cotangent):
    parent_row = parent.reshape(1, ROWS)
    gain = ln_gain.reshape(1, C1)
    raised, proj, scale, att = forward_call(counts, feats, gain, w_qkv)
    parts = backward_call(
        counts, parent_row, gain, att, feats, w_out, cotangent, w_qkv, w_down, w_up,
        proj, scale, raised,
    )
    result, d_feats, grad_qkv, grad_out, grad_down, grad_up = finish_call(*parts)
    return (result, d_feats, grad_qkv, grad_out, grad_down, grad_up.reshape(C2, C1))


def solution(mesh):
    rows = P(("pts", "grp"), None)
    line = P(("pts", "grp"))
    return jax.shard_map(
        per_device,
        mesh=mesh,
        in_specs=(rows, line, line, P(), P(), P(), P(), P(), rows),
        out_specs=(rows, rows, P(), P(), P(), P()),
        check_vma=False,
    )
```

```python
import jax
import jax.numpy as jnp
from jax import lax
from jax.experimental import pallas as pl
from jax.experimental.pallas import tpu as pltpu
from jax.sharding import PartitionSpec as P

HD = 16
HEADS = 16
ROWS = 1024
C1 = 256
C2 = 512
CORE = 256
SPILL = 64
TABLE = CORE + SPILL
EDGE = 2 * SPILL
PAIR = 2
STEPS = HEADS // PAIR
HALF = 128
BAND = 64
BANDS = C1 // BAND
SAFE_SCORE = 60.0
MESH = pl.DeviceIdType.MESH
BF = jnp.bfloat16
F32 = jnp.float32


def dg(left, right, left_dim, right_dim):
    return lax.dot_general(
        left,
        right,
        (((left_dim,), (right_dim,)), ((), ())),
        preferred_element_type=F32,
    )


def iota(shape, dim):
    return lax.broadcasted_iota(jnp.int32, shape, dim)


def norm_parts(wide):
    center = wide - jnp.mean(wide, axis=-1, keepdims=True)
    spread = jnp.mean(center * center, axis=-1, keepdims=True)
    inverse = lax.rsqrt(spread + 1e-05)
    return center * inverse, inverse


def device_number():
    return lax.axis_index("pts") * lax.axis_size("grp") + lax.axis_index("grp")


def whole(shape):
    return pl.BlockSpec(shape, lambda i, n=len(shape): (0,) * n)


def per_pair(rows):
    return pl.BlockSpec((PAIR, rows, ROWS), lambda i: (i, 0, 0))


def forward_kernel(
    counts_ref, feats_ref, gain_ref, w_qkv_ref,
    raised_hbm, proj_hbm, scale_ref, att_ref,
    proj_ref, raised_s, keys_s, query_s, mixed_s, safe_s, store_sem, proj_sem,
):
    step = pl.program_id(0)
    live = counts_ref[0]
    slot = lax.rem(step, 2)
    store_proj = pltpu.make_async_copy(proj_ref, proj_hbm, proj_sem.at[0])

    def store(at, one):
        place = lax.rem(at, 2)
        return pltpu.make_async_copy(
            raised_s.at[place, one], raised_hbm.at[at * PAIR + one], store_sem.at[place, one]
        )

    @pl.when(step == 0)
    def _():
        xhat, _ = norm_parts(feats_ref[...].astype(F32))
        normed = (xhat * gain_ref[...]).astype(BF)
        proj = dg(w_qkv_ref[...], normed, 0, 1).astype(BF)
        proj_ref[...] = proj
        store_proj.start()
        keys = dg(normed, w_qkv_ref[:, C1 : 2 * C1], 1, 0).astype(BF)
        dead = (iota((ROWS, BAND), 0) >= live) & (iota((ROWS, BAND), 1) == 0)
        bias = jnp.where(dead, -1e30, 0.0).astype(BF)
        for band in range(BANDS):
            keys_s[band] = jnp.concatenate(
                [keys[:, band * BAND : (band + 1) * BAND], bias], axis=1
            )
        ones = jnp.where(iota((BAND, ROWS), 0) == 0, 1.0, 0.0).astype(BF)
        for one in range(PAIR):
            query_s[one, BAND:, :] = ones
        wide = proj[: 2 * C1, :].astype(F32)
        squares = jnp.sum((wide * wide).reshape(2, HEADS, HD, ROWS), axis=2)
        bound = jnp.max(squares[0]) * jnp.max(squares[1]) / HD
        safe_s[0] = (bound <= SAFE_SCORE * SAFE_SCORE).astype(jnp.int32)

    band = step // (STEPS // BANDS)
    for one in range(PAIR):
        head = step * PAIR + one
        start = pl.multiple_of(head * HD, HD)
        place = pl.multiple_of(lax.rem(head, BAND // HD) * HD, HD)
        query_s[one, :BAND, :] = jnp.zeros((BAND, ROWS), BF)
        query_s[one, pl.ds(place, HD), :] = proj_ref[pl.ds(start, HD), :] * jnp.asarray(
            HD ** (-0.5), BF
        )

    @pl.when(step >= 2)
    def _():
        for one in range(PAIR):
            store(step - 2, one).wait()

    def attend(one, shifted):
        scores = dg(keys_s[band], query_s[one], 1, 0)
        if shifted:
            scores = scores - jnp.max(scores, axis=0, keepdims=True)
        raised = jnp.exp(scores)
        scale = 1.0 / jnp.sum(raised, axis=0, keepdims=True)
        raised_b = raised.astype(BF)
        raised_s[slot, one] = raised_b
        start = pl.multiple_of((step * PAIR + one) * HD, HD)
        mixed_s[one] = dg(proj_ref[pl.ds(2 * C1 + start, HD), :], raised_b, 1, 0) * scale
        scale_ref[one] = jnp.broadcast_to(scale, (8, ROWS))
        store(step, one).start()

    @pl.when(safe_s[0] == 1)
    def _():
        for one in range(PAIR):
            attend(one, False)

    @pl.when(safe_s[0] != 1)
    def _():
        for one in range(PAIR):
            attend(one, True)

    for one in range(PAIR):
        start = pl.multiple_of((step * PAIR + one) * HD, HD)
        att_ref[pl.ds(start, HD), :] = mixed_s[one].astype(BF)

    @pl.when(step == STEPS - 1)
    def _():
        store_proj.wait()
        for one in range(PAIR):
            store(step - 1, one).wait()
            store(step, one).wait()


def forward_call(counts, feats, gain, w_qkv):
    out = jax.ShapeDtypeStruct
    return pl.pallas_call(
        forward_kernel,
        grid=(STEPS,),
        in_specs=[
            pl.BlockSpec(memory_space=pltpu.SMEM),
            whole((ROWS, C1)),
            whole((1, C1)),
            whole((C1, 3 * C1)),
        ],
        out_specs=[
            pl.BlockSpec(memory_space=pl.ANY),
            pl.BlockSpec(memory_space=pl.ANY),
            per_pair(8),
            whole((C1, ROWS)),
        ],
        out_shape=[
            out((HEADS, ROWS, ROWS), BF),
            out((3 * C1, ROWS), BF),
            out((HEADS, 8, ROWS), F32),
            out((C1, ROWS), BF),
        ],
        scratch_shapes=[
            pltpu.VMEM((3 * C1, ROWS), BF),
            pltpu.VMEM((2, PAIR, ROWS, ROWS), BF),
            pltpu.VMEM((BANDS, ROWS, HALF), BF),
            pltpu.VMEM((PAIR, HALF, ROWS), BF),
            pltpu.VMEM((PAIR, HD, ROWS), F32),
            pltpu.SMEM((1,), jnp.int32),
            pltpu.SemaphoreType.DMA((2, PAIR)),
            pltpu.SemaphoreType.DMA((1,)),
        ],
        compiler_params=pltpu.CompilerParams(vmem_limit_bytes=56 * 2**20),
        name="forward",
    )(counts, feats, gain, w_qkv)


def gelu_and_slope(pre):
    root = 0.7978845608028654
    square = pre * pre
    tanh = jnp.tanh(root * (pre + 0.044715 * (square * pre)))
    value = pre * (0.5 * (1.0 + tanh))
    slope = 0.5 * (1.0 + tanh) + 0.5 * pre * (1.0 - tanh * tanh) * root * (
        1.0 + 3 * 0.044715 * square
    )
    return value, slope


def neighbour(distance):
    devices = lax.axis_size("pts") * lax.axis_size("grp")
    other = lax.rem(device_number() + distance + devices, devices)
    return (other // lax.axis_size("grp"), lax.rem(other, lax.axis_size("grp")))


GROUP = 16
UP_W = 2 * C1 + HALF
EARLY_HEADS, LATE_HEADS, LAST_HEADS = 4, 10, 2
GRADS_W = 2 * C1 + HALF
EARLY_W = GRADS_W + EARLY_HEADS * 24
LATE_W, LAST_W = LATE_HEADS * 24, LAST_HEADS * 48
EARLY_ROW, LATE_ROW, LAST_ROW = 0, 5, 10
SERVICES = (
    (4, "early", -1), (5, "early", 0), (9, "early", 1), (13, "early", 2),
    (14, "late", -1), (15, "late", 0),
)


FAR_FIRST = {
    2: (1,),
    8: (4, 3, 5, 2, 6, 1, 7),
    "plane": (10, 9, 11, 6, 14, 8, 2, 5, 7, 13, 15, 1, 3, 4, 12),
    "line": (8, 9, 7, 6, 10, 5, 11, 4, 12, 3, 13, 2, 14, 1, 15),
}


class Places:
    def __init__(self):
        pts, self.y = lax.axis_index("pts"), lax.axis_index("grp")
        self.core = lax.rem(pts, 2)
        self.x = lax.rem(pts // 2, 4)
        self.z = pts // 8
        self.plane = self.x * 4 + self.y
        self.line = self.z * 2 + self.core

    def core_peer(self, j):
        return (self.z * 8 + self.x * 2 + j, self.y)

    def plane_peer(self, j):
        return (self.z * 8 + (j // 4) * 2 + self.core, lax.rem(j, 4))

    def column_peer(self, j):
        return (j * 8 + self.x * 2 + self.core, self.y)

    def line_peer(self, j):
        return ((j // 2) * 8 + self.x * 2 + lax.rem(j, 2), self.y)


class Exchange:
    def __init__(self, places, sems, row, members, me, peer, src, slots):
        self.places = places
        self.send, self.recv = sems
        self.row, self.members, self.me, self.peer = row, members, me, peer
        self.src, self.slots = src, slots

    def copy(self, src, dst, k):
        return pltpu.make_async_remote_copy(
            src,
            dst,
            self.send.at[self.row],
            self.recv.at[self.row],
            device_id=self.peer(lax.rem(self.me + k, self.members)),
            device_id_type=MESH,
        )

    def start(self):
        if self.members == GROUP:
            order = FAR_FIRST["line" if self.peer == self.places.line_peer else "plane"]
        else:
            order = FAR_FIRST[self.members]
        for k in order:
            src = self.src(lax.rem(self.me + k, self.members))
            self.copy(src, self.slots.at[self.me], k).start()

    def whole(self):
        others = self.slots.at[pl.ds(0, self.members - 1)]
        return self.copy(others, others, 1)

    def wait(self):
        self.whole().wait_recv()

    def drain(self):
        self.whole().wait_send()


def add_slots(ref):
    return jnp.sum(ref[...].astype(F32), axis=0).astype(BF)


class FiveStep:
    def __init__(self, places, sems, row, data, pair, half, got, line, full):
        core, plane = places.core, places.plane
        self.places, self.data, self.pair, self.half = places, data, pair, half
        self.got, self.line, self.full = got, line, full
        self.stages = [
            Exchange(places, sems, row, 2, core, places.core_peer,
                     lambda j: data.at[j], pair),
            Exchange(places, sems, row + 1, GROUP, plane, places.plane_peer,
                     lambda j: half.at[j], got),
            Exchange(places, sems, row + 2, 8, places.z, places.column_peer,
                     lambda j: line.at[places.z], line),
            Exchange(places, sems, row + 3, GROUP, plane, places.plane_peer,
                     lambda j: full.at[core, plane], full.at[core]),
            Exchange(places, sems, row + 4, 2, core, places.core_peer,
                     lambda j: full.at[core], full),
        ]

    def begin(self):
        self.stages[0].start()

    def advance(self, stage):
        places = self.places
        core, plane = places.core, places.plane
        self.stages[stage].wait()
        if stage == 0:
            self.half[...] = (
                self.data[core].astype(F32) + self.pair[1 - core].astype(F32)
            ).astype(BF)
            self.got[plane] = self.half[plane]
        if stage == 1:
            self.line[places.z] = add_slots(self.got)
        if stage == 2:
            self.full[core, plane] = add_slots(self.line)
        if stage < 4:
            self.stages[stage + 1].start()


class ThreeStep:
    def __init__(self, places, sems, row, data, got, line, full):
        plane = places.plane
        self.places, self.data, self.got = places, data, got
        self.line, self.full = line, full
        self.stages = [
            Exchange(places, sems, row, GROUP, plane, places.plane_peer,
                     lambda j: data.at[j], got),
            Exchange(places, sems, row + 1, GROUP, places.line, places.line_peer,
                     lambda j: line.at[places.line], line),
            Exchange(places, sems, row + 2, GROUP, plane, places.plane_peer,
                     lambda j: full.at[plane], full),
        ]

    def begin(self):
        plane = self.places.plane
        self.stages[0].start()
        self.got[plane] = self.data[plane]

    def advance(self, stage):
        places = self.places
        self.stages[stage].wait()
        if stage == 0:
            self.line[places.line] = add_slots(self.got)
        if stage == 1:
            self.full[places.plane] = add_slots(self.line)
        if stage < 2:
            self.stages[stage + 1].start()


def backward_kernel(
    counts_ref, parent_ref, gain_ref,
    att_hbm, feats_hbm, w_out_hbm, cot_hbm, w_qkv_hbm, w_down_hbm, w_up_hbm, proj_hbm, scale_hbm,
    raised_hbm,
    result_hbm, d_feats_hbm, early_hbm, late_hbm, last_hbm,
    att_ref, feats_ref, w_out_ref, cot_ref, w_qkv_ref, w_down_ref, w_up_ref, proj_ref, scale_ref,
    result_s, d_feats_s, raised_s, hidden_s, sum_s,
    d_hidden_s, normed_s, across_s, d_att_s, d_proj_s, values_s, cots_s, member_s, back_s,
    send_up, recv_up, send_down, recv_down,
    e_data, e_pair, e_half, e_got, e_line, e_full,
    f_data, f_pair, f_half, f_got, f_line, f_full,
    t_data, t_got, t_line, t_full,
    near_send, near_recv, far_send, far_recv, load_sem, raised_sem, store_sem,
):
    step = pl.program_id(0)
    live = counts_ref[0]
    places = Places()
    sems = (far_send, far_recv)
    early = FiveStep(places, sems, EARLY_ROW, e_data, e_pair, e_half, e_got, e_line, e_full)
    late = FiveStep(places, sems, LATE_ROW, f_data, f_pair, f_half, f_got, f_line, f_full)
    last = ThreeStep(places, sems, LAST_ROW, t_data, t_got, t_line, t_full)
    chunks = {"early": early, "late": late}
    loads = [
        pltpu.make_async_copy(src, dst, load_sem.at[n])
        for n, (src, dst) in enumerate(
            (
                (att_hbm, att_ref), (feats_hbm, feats_ref), (w_out_hbm, w_out_ref),
                (cot_hbm, cot_ref), (w_qkv_hbm, w_qkv_ref), (w_down_hbm, w_down_ref),
                (w_up_hbm, w_up_ref), (proj_hbm, proj_ref), (scale_hbm, scale_ref),
            )
        )
    ]
    stores = [
        pltpu.make_async_copy(src, dst, store_sem.at[n])
        for n, (src, dst) in enumerate(
            (
                (result_s, result_hbm), (d_feats_s, d_feats_hbm), (e_full, early_hbm),
                (f_full, late_hbm), (t_full, last_hbm),
            )
        )
    ]

    after, before = neighbour(1), neighbour(-1)
    near = [
        pltpu.make_async_remote_copy(
            src, dst, near_send.at[n], near_recv.at[n], device_id=other, device_id_type=MESH
        )
        for n, (src, dst, other) in enumerate(
            ((send_up, recv_up, after), (send_down, recv_down, before))
        )
    ]

    def load_raised(at):
        slot = lax.rem(at, 2)
        return pltpu.make_async_copy(
            raised_hbm.at[pl.ds(at * PAIR, PAIR)], raised_s.at[slot], raised_sem.at[slot]
        )

    @pl.when(step == 0)
    def _():
        barrier = pltpu.get_barrier_semaphore()
        for other in (after, before):
            pl.semaphore_signal(barrier, inc=1, device_id=other, device_id_type=MESH)
        for load in loads[:4]:
            load.start()
        for in_plane, in_line in zip(FAR_FIRST["plane"], FAR_FIRST["line"]):
            for other in (
                places.plane_peer(lax.rem(places.plane + in_plane, GROUP)),
                places.line_peer(lax.rem(places.line + in_line, GROUP)),
            ):
                pl.semaphore_signal(barrier, inc=1, device_id=other, device_id_type=MESH)
        for load in loads[4:7]:
            load.start()
        for load in loads[7:]:
            load.start()
        load_raised(0).start()
        for load in loads[:4]:
            load.wait()

        attended = att_ref[...].T
        hidden = (
            feats_ref[...].astype(F32) + dg(attended, w_out_ref[...], 1, 0)
        ).astype(BF)
        hidden_s[...] = hidden
        local = parent_ref[...] - device_number() * CORE
        local = jnp.where(
            local < SPILL,
            local,
            jnp.where(local < CORE, local + SPILL, local - (CORE - SPILL)),
        )
        member = (local == iota((TABLE, ROWS), 0)) & (iota((TABLE, ROWS), 1) < live)
        member_f = jnp.where(member, 1.0, 0.0)
        counted = jnp.sum(member_f, axis=1, keepdims=True)
        sum_s[:, :C1] = dg(member_f.astype(BF), hidden, 1, 0)
        sum_s[:, C1 : 2 * C1] = dg(member_f.astype(BF), cot_ref[...], 1, 0)
        sum_s[:, 2 * C1 :] = jnp.broadcast_to(counted, (TABLE, HALF))
        for buf, rows in ((send_up, slice(SPILL, EDGE)), (send_down, slice(0, SPILL))):
            buf[:, : 2 * C1] = sum_s[rows, : 2 * C1].astype(BF)
            count = sum_s[rows, 2 * C1 :]
            high = count.astype(BF)
            low = (count - high.astype(F32)).astype(BF)
            buf[:, 2 * C1 :] = jnp.where(iota((SPILL, HALF), 1) < HALF // 2, high, low)
        pl.semaphore_wait(barrier, 2 * GROUP)
        for copy in near:
            copy.start()

        for load in loads[4:7]:
            load.wait()
        xhat, _ = norm_parts(feats_ref[...].astype(F32))
        normed = (xhat * gain_ref[...]).astype(BF)
        normed_s[...] = normed
        across_s[...] = normed.T
        values = dg(normed, w_qkv_ref[:, 2 * C1 :], 1, 0).astype(BF)
        ones = jnp.where(iota((ROWS, BAND), 1) < 2, 1.0, 0.0).astype(BF)
        for band in range(BANDS):
            values_s[band] = jnp.concatenate(
                [values[:, band * BAND : (band + 1) * BAND], ones], axis=1
            )
        for one in range(PAIR):
            cots_s[one] = jnp.zeros((HALF, ROWS), BF)
        column = jnp.broadcast_to(local.astype(F32), (HALF, ROWS)).T[:, :1].astype(jnp.int32)
        member = (column == iota((ROWS, TABLE), 1)) & (iota((ROWS, TABLE), 0) < live)
        member_s[...] = jnp.where(member, 1.0, 0.0).astype(BF)

        def coarse(total, total_cot, counted):
            inverse = 1.0 / jnp.maximum(counted, 1.0)
            pooled = (total * inverse).astype(BF)
            value, slope = gelu_and_slope(dg(pooled, w_down_ref[...], 1, 0))
            activ = value.astype(BF)
            back = dg(activ, w_up_ref[...], 1, 0).astype(BF)
            d_back = total_cot.astype(BF)
            d_pre = (dg(d_back, w_up_ref[...], 1, 1) * slope).astype(BF)
            share = dg(d_pre, w_down_ref[...], 1, 1) * inverse
            high = share.astype(BF)
            low = (share - high.astype(F32)).astype(BF)
            return pooled, activ, back, d_back, d_pre, high, low

        middle = slice(EDGE, TABLE)
        pooled, activ, back, d_back, d_pre, high, low = coarse(
            sum_s[middle, :C1],
            sum_s[middle, C1 : 2 * C1],
            sum_s[middle, 2 * C1 : 2 * C1 + 1],
        )
        back_s[middle, :] = back
        grad_up = dg(activ, d_back, 0, 0)
        grad_down = dg(pooled, d_pre, 0, 0)
        inner = member_s[:, middle]
        d_hidden_s[...] = (
            cot_ref[...].astype(F32) + dg(inner, high, 1, 0) + dg(inner, low, 1, 0)
        )

        for copy in near:
            copy.wait_recv()
        got = jnp.concatenate([recv_up[...], recv_down[...]], axis=0).astype(F32)
        count_in = (
            got[:, 2 * C1 : 2 * C1 + 1]
            + got[:, 2 * C1 + HALF // 2 : 2 * C1 + HALF // 2 + 1]
        )
        pooled, activ, back, d_back, d_pre, high, low = coarse(
            sum_s[:EDGE, :C1] + got[:, :C1],
            sum_s[:EDGE, C1 : 2 * C1] + got[:, C1 : 2 * C1],
            sum_s[:EDGE, 2 * C1 : 2 * C1 + 1] + count_in,
        )
        outer = member_s[:, :EDGE]
        d_hidden = (
            d_hidden_s[...]
            + dg(
                jnp.concatenate([outer, outer], axis=1),
                jnp.concatenate([high, low], axis=0),
                1,
                0,
            )
        )
        d_hidden_s[...] = d_hidden
        d_hidden_b = d_hidden.astype(BF)
        d_att_s[...] = dg(w_out_ref[...], d_hidden_b, 1, 1).astype(BF)
        back_s[:EDGE, :] = back
        grad_up = (grad_up + dg(activ[:SPILL], d_back[:SPILL], 0, 0)).astype(BF)
        grad_up = grad_up.reshape(GROUP, 2, 16, C1)
        grad_down = (grad_down + dg(pooled[:SPILL], d_pre[:SPILL], 0, 0)).astype(BF)
        grad_down = grad_down.reshape(GROUP, 16, C2)
        for core in range(2):
            e_data[core, :, :, :C1] = grad_up[:, core]
            e_data[core, :, :, C1 : 2 * C1] = grad_down[:, :, core * C1 : (core + 1) * C1]
        grad_out = dg(att_ref[...], d_hidden_b, 1, 0).astype(BF).reshape(GROUP, 16, C1)
        for core in range(2):
            e_data[core, :, :, 2 * C1 : GRADS_W] = grad_out[:, :, core * HALF : (core + 1) * HALF]
        for load in loads[7:]:
            load.wait()

    @pl.when(step < STEPS - 1)
    def _():
        load_raised(step + 1).start()

    load_raised(step).wait()

    def grad_columns(head, heads):
        rows = [
            d_proj_s[part * C1 + head * HD : part * C1 + (head + heads) * HD, :]
            for part in range(3)
        ]
        return dg(across_s[...], jnp.concatenate(rows, axis=0), 1, 1).astype(BF)

    def fill_halves(data, first, head, heads):
        grads = grad_columns(head, heads)
        width = 3 * heads * HD // 2
        for core in range(2):
            data[core, :, :, first : first + width] = grads[
                :, core * width : (core + 1) * width
            ].reshape(GROUP, 16, width)

    def serve(name, stage):
        if stage >= 0:
            chunks[name].advance(stage)
            return
        if name == "early":
            fill_halves(e_data, GRADS_W, 0, EARLY_HEADS)
        else:
            fill_halves(f_data, 0, EARLY_HEADS, LATE_HEADS)
        chunks[name].begin()

    band = step // (STEPS // BANDS)
    quarter = jnp.asarray(HD ** (-0.5), BF)
    for one in range(PAIR):
        for turn, name, stage in SERVICES:
            if turn % PAIR == one:
                @pl.when(step == turn // PAIR)
                def _(name=name, stage=stage):
                    serve(name, stage)

        head = step * PAIR + one
        start = pl.multiple_of(head * HD, HD)
        place = pl.multiple_of(lax.rem(head, BAND // HD) * HD, HD)
        cot = (d_att_s[pl.ds(start, HD), :].astype(F32) * scale_ref[head, :1, :]).astype(BF)
        inner = -jnp.sum(
            cot.astype(F32) * att_ref[pl.ds(start, HD), :].astype(F32), axis=0, keepdims=True
        )
        high = inner.astype(BF).astype(F32)
        rows = iota((HD, ROWS), 0)
        cots_s[one, :BAND, :] = jnp.zeros((BAND, ROWS), BF)
        cots_s[one, pl.ds(place, HD), :] = cot
        cots_s[one, BAND : BAND + HD, :] = jnp.where(
            rows == 0, high, jnp.where(rows == 1, inner - high, 0.0)
        ).astype(BF)
        raised = raised_s[lax.rem(step, 2), one]
        d_scores = raised * dg(values_s[band], cots_s[one], 1, 0).astype(BF)
        d_proj_s[pl.ds(start, HD), :] = dg(
            proj_ref[pl.ds(C1 + start, HD), :] * quarter, d_scores, 1, 0
        ).astype(BF)
        d_proj_s[pl.ds(2 * C1 + start, HD), :] = dg(cot, raised, 1, 1).astype(BF)
        d_proj_s[pl.ds(C1 + start, HD), :] = dg(
            proj_ref[pl.ds(start, HD), :] * quarter, d_scores, 1, 1
        ).astype(BF)

    @pl.when(step == STEPS - 1)
    def _():
        grads = grad_columns(EARLY_HEADS + LATE_HEADS, LAST_HEADS)
        t_data[...] = grads.reshape(GROUP, 16, LAST_W)
        last.begin()
        d_normed = dg(w_qkv_ref[...], d_proj_s[...], 1, 0).T
        early.advance(3)
        late.advance(1)
        xhat, inverse = norm_parts(feats_ref[...].astype(F32))
        grown = d_normed * gain_ref[...]
        along = jnp.mean(grown * xhat, axis=-1, keepdims=True)
        d_wide = inverse * (grown - jnp.mean(grown, axis=-1, keepdims=True) - xhat * along)
        d_feats_s[...] = (d_hidden_s[...] + d_wide).astype(BF)
        stores[1].start()
        last.advance(0)
        early.advance(4)
        stores[2].start()
        result_s[...] = (
            hidden_s[...].astype(F32) + dg(member_s[...], back_s[...], 1, 0)
        ).astype(BF)
        stores[0].start()
        late.advance(2)
        last.advance(1)
        late.advance(3)
        late.advance(4)
        stores[3].start()
        last.advance(2)
        stores[4].start()
        for chunk in (early, late, last):
            for stage in chunk.stages:
                stage.drain()
        for copy in near:
            copy.wait_send()
        for store in stores:
            store.wait()


def backward_call(counts, parent, gain, att, feats, w_out, cotangent, w_qkv, w_down, w_up,
                  proj, scale, raised):
    out = jax.ShapeDtypeStruct
    vmem = pltpu.VMEM
    anywhere = pl.BlockSpec(memory_space=pl.ANY)
    early, late, last = (
        (2, GROUP, 16, EARLY_W),
        (2, GROUP, 16, LATE_W),
        (GROUP, 16, LAST_W),
    )
    loaded = (att, feats, w_out, cotangent, w_qkv, w_down, w_up, proj, scale)

    def five(shape):
        return [
            vmem(shape, BF), vmem(shape, BF), vmem(shape[1:], BF), vmem(shape[1:], BF),
            vmem((8,) + shape[2:], BF), vmem(shape, BF),
        ]

    return pl.pallas_call(
        backward_kernel,
        grid=(STEPS,),
        in_specs=[
            pl.BlockSpec(memory_space=pltpu.SMEM),
            whole((1, ROWS)),
            whole((1, C1)),
        ]
        + [anywhere] * 10,
        out_specs=[anywhere] * 5,
        out_shape=[
            out((ROWS, C1), BF),
            out((ROWS, C1), BF),
            out(early, BF),
            out(late, BF),
            out(last, BF),
        ],
        scratch_shapes=[vmem(array.shape, array.dtype) for array in loaded]
        + [
            vmem((ROWS, C1), BF),
            vmem((ROWS, C1), BF),
            vmem((2, PAIR, ROWS, ROWS), BF),
            vmem((ROWS, C1), BF),
            vmem((TABLE, UP_W), F32),
            vmem((ROWS, C1), F32),
            vmem((ROWS, C1), BF),
            vmem((C1, ROWS), BF),
            vmem((C1, ROWS), BF),
            vmem((3 * C1, ROWS), BF),
            vmem((BANDS, ROWS, HALF), BF),
            vmem((PAIR, HALF, ROWS), BF),
            vmem((ROWS, TABLE), BF),
            vmem((TABLE, C1), BF),
            vmem((SPILL, UP_W), BF),
            vmem((SPILL, UP_W), BF),
            vmem((SPILL, UP_W), BF),
            vmem((SPILL, UP_W), BF),
        ]
        + five(early)
        + five(late)
        + [vmem(last, BF)] * 4
        + [
            pltpu.SemaphoreType.DMA((2,)),
            pltpu.SemaphoreType.DMA((2,)),
            pltpu.SemaphoreType.DMA((13,)),
            pltpu.SemaphoreType.DMA((13,)),
            pltpu.SemaphoreType.DMA((9,)),
            pltpu.SemaphoreType.DMA((2,)),
            pltpu.SemaphoreType.DMA((5,)),
        ],
        compiler_params=pltpu.CompilerParams(
            collective_id=0, has_side_effects=True, vmem_limit_bytes=58 * 2**20
        ),
        name="backward",
    )(counts, parent, gain, *loaded, raised)


def finish_kernel(
    result_hbm, d_feats_hbm, early_hbm, late_hbm, last_hbm,
    result_out, d_feats_out, qkv_out, out_out, down_out, up_out,
    result_s, d_feats_s, early_ref, late_ref, last_ref, qkv_s, out_s, down_s, up_s, load_sem, pass_sem, store_sem,
):
    loads = [
        pltpu.make_async_copy(src, dst, load_sem.at[n])
        for n, (src, dst) in enumerate(
            (
                (early_hbm, early_ref), (late_hbm, late_ref), (last_hbm, last_ref),
                (result_hbm, result_s), (d_feats_hbm, d_feats_s),
            )
        )
    ]
    passes = [
        pltpu.make_async_copy(result_s, result_out, pass_sem.at[0]),
        pltpu.make_async_copy(d_feats_s, d_feats_out, pass_sem.at[1]),
    ]
    stores = [
        pltpu.make_async_copy(src, dst, store_sem.at[n])
        for n, (src, dst) in enumerate(
            ((qkv_s, qkv_out), (out_s, out_out), (down_s, down_out), (up_s, up_out))
        )
    ]
    for load in loads:
        load.start()
    loads[0].wait()
    for core in range(2):
        up_s[:, core] = early_ref[core, :, :, :C1].astype(F32)
        down_s[:, core * C1 : (core + 1) * C1] = (
            early_ref[core, :, :, C1 : 2 * C1].reshape(C1, C1).astype(F32)
        )
        out_s[:, core * HALF : (core + 1) * HALF] = (
            early_ref[core, :, :, 2 * C1 : GRADS_W].reshape(C1, HALF).astype(F32)
        )
    for store in stores[1:]:
        store.start()
    for load in loads[1:]:
        load.wait()
    for one in passes:
        one.start()
    early, late = [
        jnp.concatenate(
            [ref[core, :, :, first:].astype(F32).reshape(C1, -1) for core in range(2)], axis=1
        )
        for ref, first in ((early_ref, GRADS_W), (late_ref, 0))
    ]
    last = last_ref[...].astype(F32).reshape(C1, LAST_W)
    for part in range(3):
        qkv_s[:, part * C1 : (part + 1) * C1] = jnp.concatenate(
            [
                piece[:, part * heads * HD : (part + 1) * heads * HD]
                for piece, heads in (
                    (early, EARLY_HEADS), (late, LATE_HEADS), (last, LAST_HEADS)
                )
            ],
            axis=1,
        )
    stores[0].start()
    for copy in passes + stores:
        copy.wait()


def finish_call(*parts):
    anywhere = pl.BlockSpec(memory_space=pl.ANY)
    shapes = [
        ((ROWS, C1), BF), ((ROWS, C1), BF), ((C1, 3 * C1), F32), ((C1, C1), F32),
        ((C1, C2), F32), ((GROUP, 2, 16, C1), F32),
    ]
    return pl.pallas_call(
        finish_kernel,
        in_specs=[anywhere] * 5,
        out_specs=[anywhere] * 6,
        out_shape=[jax.ShapeDtypeStruct(shape, kind) for shape, kind in shapes],
        scratch_shapes=[pltpu.VMEM(part.shape, BF) for part in parts]
        + [pltpu.VMEM(shape, F32) for shape, _ in shapes[2:]]
        + [
            pltpu.SemaphoreType.DMA((5,)),
            pltpu.SemaphoreType.DMA((2,)),
            pltpu.SemaphoreType.DMA((4,)),
        ],
        compiler_params=pltpu.CompilerParams(vmem_limit_bytes=60 * 2**20),
        name="finish",
    )(*parts)


def per_device(feats, counts, parent, ln_gain, w_qkv, w_out, w_down, w_up, cotangent):
    parent_row = parent.reshape(1, ROWS)
    gain = ln_gain.reshape(1, C1)
    raised, proj, scale, att = forward_call(counts, feats, gain, w_qkv)
    parts = backward_call(
        counts, parent_row, gain, att, feats, w_out, cotangent, w_qkv, w_down, w_up,
        proj, scale, raised,
    )
    result, d_feats, grad_qkv, grad_out, grad_down, grad_up = finish_call(*parts)
    return (result, d_feats, grad_qkv, grad_out, grad_down, grad_up.reshape(C2, C1))


def solution(mesh):
    rows = P(("pts", "grp"), None)
    line = P(("pts", "grp"))
    return jax.shard_map(
        per_device,
        mesh=mesh,
        in_specs=(rows, line, line, P(), P(), P(), P(), P(), rows),
        out_specs=(rows, rows, P(), P(), P(), P()),
        check_vma=False,
    )
```

```python
import jax
import jax.numpy as jnp
from jax import lax
from jax.experimental import pallas as pl
from jax.experimental.pallas import tpu as pltpu
from jax.sharding import PartitionSpec as P

HD = 16
HEADS = 16
ROWS = 1024
C1 = 256
C2 = 512
CORE = 256
SPILL = 64
TABLE = CORE + SPILL
EDGE = 2 * SPILL
PAIR = 2
STEPS = HEADS // PAIR
HALF = 128
BAND = 64
BANDS = C1 // BAND
SAFE_SCORE = 60.0
MESH = pl.DeviceIdType.MESH
BF = jnp.bfloat16
F32 = jnp.float32


def dg(left, right, left_dim, right_dim):
    return lax.dot_general(
        left,
        right,
        (((left_dim,), (right_dim,)), ((), ())),
        preferred_element_type=F32,
    )


def iota(shape, dim):
    return lax.broadcasted_iota(jnp.int32, shape, dim)


def norm_parts(wide):
    center = wide - jnp.mean(wide, axis=-1, keepdims=True)
    spread = jnp.mean(center * center, axis=-1, keepdims=True)
    inverse = lax.rsqrt(spread + 1e-05)
    return center * inverse, inverse


def device_number():
    return lax.axis_index("pts") * lax.axis_size("grp") + lax.axis_index("grp")


def whole(shape):
    return pl.BlockSpec(shape, lambda i, n=len(shape): (0,) * n)


def per_pair(rows):
    return pl.BlockSpec((PAIR, rows, ROWS), lambda i: (i, 0, 0))


def forward_kernel(
    counts_ref, feats_ref, gain_ref, w_qkv_ref,
    raised_hbm, proj_hbm, scale_ref, att_ref,
    proj_ref, raised_s, keys_s, query_s, mixed_s, safe_s, store_sem, proj_sem,
):
    step = pl.program_id(0)
    live = counts_ref[0]
    slot = lax.rem(step, 2)
    store_proj = pltpu.make_async_copy(proj_ref, proj_hbm, proj_sem.at[0])

    def store(at, one):
        place = lax.rem(at, 2)
        return pltpu.make_async_copy(
            raised_s.at[place, one], raised_hbm.at[at * PAIR + one], store_sem.at[place, one]
        )

    @pl.when(step == 0)
    def _():
        xhat, _ = norm_parts(feats_ref[...].astype(F32))
        normed = (xhat * gain_ref[...]).astype(BF)
        proj = dg(w_qkv_ref[...], normed, 0, 1).astype(BF)
        proj_ref[...] = proj
        store_proj.start()
        keys = dg(normed, w_qkv_ref[:, C1 : 2 * C1], 1, 0).astype(BF)
        dead = (iota((ROWS, BAND), 0) >= live) & (iota((ROWS, BAND), 1) == 0)
        bias = jnp.where(dead, -1e30, 0.0).astype(BF)
        for band in range(BANDS):
            keys_s[band] = jnp.concatenate(
                [keys[:, band * BAND : (band + 1) * BAND], bias], axis=1
            )
        ones = jnp.where(iota((BAND, ROWS), 0) == 0, 1.0, 0.0).astype(BF)
        for one in range(PAIR):
            query_s[one, BAND:, :] = ones
        wide = proj[: 2 * C1, :].astype(F32)
        squares = jnp.sum((wide * wide).reshape(2, HEADS, HD, ROWS), axis=2)
        bound = jnp.max(squares[0]) * jnp.max(squares[1]) / HD
        safe_s[0] = (bound <= SAFE_SCORE * SAFE_SCORE).astype(jnp.int32)

    band = step // (STEPS // BANDS)
    for one in range(PAIR):
        head = step * PAIR + one
        start = pl.multiple_of(head * HD, HD)
        place = pl.multiple_of(lax.rem(head, BAND // HD) * HD, HD)
        query_s[one, :BAND, :] = jnp.zeros((BAND, ROWS), BF)
        query_s[one, pl.ds(place, HD), :] = proj_ref[pl.ds(start, HD), :] * jnp.asarray(
            HD ** (-0.5), BF
        )

    @pl.when(step >= 2)
    def _():
        for one in range(PAIR):
            store(step - 2, one).wait()

    def attend(one, shifted):
        scores = dg(keys_s[band], query_s[one], 1, 0)
        if shifted:
            scores = scores - jnp.max(scores, axis=0, keepdims=True)
        raised = jnp.exp(scores)
        scale = 1.0 / jnp.sum(raised, axis=0, keepdims=True)
        raised_b = raised.astype(BF)
        raised_s[slot, one] = raised_b
        start = pl.multiple_of((step * PAIR + one) * HD, HD)
        mixed_s[one] = dg(proj_ref[pl.ds(2 * C1 + start, HD), :], raised_b, 1, 0) * scale
        scale_ref[one] = jnp.broadcast_to(scale, (8, ROWS))
        store(step, one).start()

    @pl.when(safe_s[0] == 1)
    def _():
        for one in range(PAIR):
            attend(one, False)

    @pl.when(safe_s[0] != 1)
    def _():
        for one in range(PAIR):
            attend(one, True)

    for one in range(PAIR):
        start = pl.multiple_of((step * PAIR + one) * HD, HD)
        att_ref[pl.ds(start, HD), :] = mixed_s[one].astype(BF)

    @pl.when(step == STEPS - 1)
    def _():
        store_proj.wait()
        for one in range(PAIR):
            store(step - 1, one).wait()
            store(step, one).wait()


def forward_call(counts, feats, gain, w_qkv):
    out = jax.ShapeDtypeStruct
    return pl.pallas_call(
        forward_kernel,
        grid=(STEPS,),
        in_specs=[
            pl.BlockSpec(memory_space=pltpu.SMEM),
            whole((ROWS, C1)),
            whole((1, C1)),
            whole((C1, 3 * C1)),
        ],
        out_specs=[
            pl.BlockSpec(memory_space=pl.ANY),
            pl.BlockSpec(memory_space=pl.ANY),
            per_pair(8),
            whole((C1, ROWS)),
        ],
        out_shape=[
            out((HEADS, ROWS, ROWS), BF),
            out((3 * C1, ROWS), BF),
            out((HEADS, 8, ROWS), F32),
            out((C1, ROWS), BF),
        ],
        scratch_shapes=[
            pltpu.VMEM((3 * C1, ROWS), BF),
            pltpu.VMEM((2, PAIR, ROWS, ROWS), BF),
            pltpu.VMEM((BANDS, ROWS, HALF), BF),
            pltpu.VMEM((PAIR, HALF, ROWS), BF),
            pltpu.VMEM((PAIR, HD, ROWS), F32),
            pltpu.SMEM((1,), jnp.int32),
            pltpu.SemaphoreType.DMA((2, PAIR)),
            pltpu.SemaphoreType.DMA((1,)),
        ],
        compiler_params=pltpu.CompilerParams(vmem_limit_bytes=56 * 2**20),
        name="forward",
    )(counts, feats, gain, w_qkv)


def gelu_and_slope(pre):
    root = 0.7978845608028654
    square = pre * pre
    tanh = jnp.tanh(root * (pre + 0.044715 * (square * pre)))
    value = pre * (0.5 * (1.0 + tanh))
    slope = 0.5 * (1.0 + tanh) + 0.5 * pre * (1.0 - tanh * tanh) * root * (
        1.0 + 3 * 0.044715 * square
    )
    return value, slope


def neighbour(distance):
    devices = lax.axis_size("pts") * lax.axis_size("grp")
    other = lax.rem(device_number() + distance + devices, devices)
    return (other // lax.axis_size("grp"), lax.rem(other, lax.axis_size("grp")))


GROUP = 16
UP_W = 2 * C1 + HALF
EARLY_HEADS, LATE_HEADS, LAST_HEADS = 4, 10, 2
GRADS_W = 2 * C1 + HALF
EARLY_W = GRADS_W + EARLY_HEADS * 24
LATE_W, LAST_W = LATE_HEADS * 24, LAST_HEADS * 48
EARLY_ROW, LATE_ROW, LAST_ROW = 0, 5, 10
SERVICES = (
    (4, "early", -1), (5, "early", 0), (9, "early", 1), (13, "early", 2),
    (14, "late", -1), (15, "late", 0),
)


FAR_FIRST = {
    2: (1,),
    8: (4, 3, 5, 2, 6, 1, 7),
    "plane": (10, 9, 11, 6, 14, 8, 2, 5, 7, 13, 15, 1, 3, 4, 12),
    "line": (8, 9, 7, 6, 10, 5, 11, 4, 12, 3, 13, 2, 14, 1, 15),
}


class Places:
    def __init__(self):
        pts, self.y = lax.axis_index("pts"), lax.axis_index("grp")
        self.core = lax.rem(pts, 2)
        self.x = lax.rem(pts // 2, 4)
        self.z = pts // 8
        self.plane = self.x * 4 + self.y
        self.line = self.z * 2 + self.core

    def core_peer(self, j):
        return (self.z * 8 + self.x * 2 + j, self.y)

    def plane_peer(self, j):
        return (self.z * 8 + (j // 4) * 2 + self.core, lax.rem(j, 4))

    def column_peer(self, j):
        return (j * 8 + self.x * 2 + self.core, self.y)

    def line_peer(self, j):
        return ((j // 2) * 8 + self.x * 2 + lax.rem(j, 2), self.y)


class Exchange:
    def __init__(self, places, sems, row, members, me, peer, src, slots):
        self.places = places
        self.send, self.recv = sems
        self.row, self.members, self.me, self.peer = row, members, me, peer
        self.src, self.slots = src, slots

    def copy(self, src, dst, k):
        return pltpu.make_async_remote_copy(
            src,
            dst,
            self.send.at[self.row],
            self.recv.at[self.row],
            device_id=self.peer(lax.rem(self.me + k, self.members)),
            device_id_type=MESH,
        )

    def start(self):
        if self.members == GROUP:
            order = FAR_FIRST["line" if self.peer == self.places.line_peer else "plane"]
        else:
            order = FAR_FIRST[self.members]
        for k in order:
            src = self.src(lax.rem(self.me + k, self.members))
            self.copy(src, self.slots.at[self.me], k).start()

    def whole(self):
        others = self.slots.at[pl.ds(0, self.members - 1)]
        return self.copy(others, others, 1)

    def wait(self):
        self.whole().wait_recv()

    def drain(self):
        self.whole().wait_send()


def add_slots(ref):
    return jnp.sum(ref[...].astype(F32), axis=0).astype(BF)


class FiveStep:
    def __init__(self, places, sems, row, data, pair, half, got, line, full):
        core, plane = places.core, places.plane
        self.places, self.data, self.pair, self.half = places, data, pair, half
        self.got, self.line, self.full = got, line, full
        self.stages = [
            Exchange(places, sems, row, 2, core, places.core_peer,
                     lambda j: data.at[j], pair),
            Exchange(places, sems, row + 1, GROUP, plane, places.plane_peer,
                     lambda j: half.at[j], got),
            Exchange(places, sems, row + 2, 8, places.z, places.column_peer,
                     lambda j: line.at[places.z], line),
            Exchange(places, sems, row + 3, GROUP, plane, places.plane_peer,
                     lambda j: full.at[core, plane], full.at[core]),
            Exchange(places, sems, row + 4, 2, core, places.core_peer,
                     lambda j: full.at[core], full),
        ]

    def begin(self):
        self.stages[0].start()

    def advance(self, stage):
        places = self.places
        core, plane = places.core, places.plane
        self.stages[stage].wait()
        if stage == 0:
            self.half[...] = (
                self.data[core].astype(F32) + self.pair[1 - core].astype(F32)
            ).astype(BF)
            self.got[plane] = self.half[plane]
        if stage == 1:
            self.line[places.z] = add_slots(self.got)
        if stage == 2:
            self.full[core, plane] = add_slots(self.line)
        if stage < 4:
            self.stages[stage + 1].start()


class ThreeStep:
    def __init__(self, places, sems, row, data, got, line, full):
        plane = places.plane
        self.places, self.data, self.got = places, data, got
        self.line, self.full = line, full
        self.stages = [
            Exchange(places, sems, row, GROUP, plane, places.plane_peer,
                     lambda j: data.at[j], got),
            Exchange(places, sems, row + 1, GROUP, places.line, places.line_peer,
                     lambda j: line.at[places.line], line),
            Exchange(places, sems, row + 2, GROUP, plane, places.plane_peer,
                     lambda j: full.at[plane], full),
        ]

    def begin(self):
        plane = self.places.plane
        self.stages[0].start()
        self.got[plane] = self.data[plane]

    def advance(self, stage):
        places = self.places
        self.stages[stage].wait()
        if stage == 0:
            self.line[places.line] = add_slots(self.got)
        if stage == 1:
            self.full[places.plane] = add_slots(self.line)
        if stage < 2:
            self.stages[stage + 1].start()


def backward_kernel(
    counts_ref, parent_ref, gain_ref,
    att_hbm, feats_hbm, w_out_hbm, cot_hbm, w_qkv_hbm, w_down_hbm, w_up_hbm, proj_hbm, scale_hbm,
    raised_hbm,
    result_hbm, d_feats_hbm, early_hbm, late_hbm, last_hbm,
    att_ref, feats_ref, w_out_ref, cot_ref, w_qkv_ref, w_down_ref, w_up_ref, proj_ref, scale_ref,
    result_s, d_feats_s, raised_s, hidden_s, sum_s,
    d_hidden_s, normed_s, across_s, d_att_s, d_proj_s, values_s, cots_s, member_s, back_s,
    send_up, recv_up, send_down, recv_down,
    e_data, e_pair, e_half, e_got, e_line, e_full,
    f_data, f_pair, f_half, f_got, f_line, f_full,
    t_data, t_got, t_line, t_full,
    near_send, near_recv, far_send, far_recv, load_sem, raised_sem, store_sem,
):
    step = pl.program_id(0)
    live = counts_ref[0]
    places = Places()
    sems = (far_send, far_recv)
    early = FiveStep(places, sems, EARLY_ROW, e_data, e_pair, e_half, e_got, e_line, e_full)
    late = FiveStep(places, sems, LATE_ROW, f_data, f_pair, f_half, f_got, f_line, f_full)
    last = ThreeStep(places, sems, LAST_ROW, t_data, t_got, t_line, t_full)
    chunks = {"early": early, "late": late}
    loads = [
        pltpu.make_async_copy(src, dst, load_sem.at[n])
        for n, (src, dst) in enumerate(
            (
                (att_hbm, att_ref), (feats_hbm, feats_ref), (w_out_hbm, w_out_ref),
                (cot_hbm, cot_ref), (w_qkv_hbm, w_qkv_ref), (w_down_hbm, w_down_ref),
                (w_up_hbm, w_up_ref), (proj_hbm, proj_ref), (scale_hbm, scale_ref),
            )
        )
    ]
    stores = [
        pltpu.make_async_copy(src, dst, store_sem.at[n])
        for n, (src, dst) in enumerate(
            (
                (result_s, result_hbm), (d_feats_s, d_feats_hbm), (e_full, early_hbm),
                (f_full, late_hbm), (t_full, last_hbm),
            )
        )
    ]

    after, before = neighbour(1), neighbour(-1)
    near = [
        pltpu.make_async_remote_copy(
            src, dst, near_send.at[n], near_recv.at[n], device_id=other, device_id_type=MESH
        )
        for n, (src, dst, other) in enumerate(
            ((send_up, recv_up, after), (send_down, recv_down, before))
        )
    ]

    def load_raised(at):
        slot = lax.rem(at, 2)
        return pltpu.make_async_copy(
            raised_hbm.at[pl.ds(at * PAIR, PAIR)], raised_s.at[slot], raised_sem.at[slot]
        )

    @pl.when(step == 0)
    def _():
        barrier = pltpu.get_barrier_semaphore()
        for other in (after, before):
            pl.semaphore_signal(barrier, inc=1, device_id=other, device_id_type=MESH)
        for load in loads[:4]:
            load.start()
        for in_plane, in_line in zip(FAR_FIRST["plane"], FAR_FIRST["line"]):
            for other in (
                places.plane_peer(lax.rem(places.plane + in_plane, GROUP)),
                places.line_peer(lax.rem(places.line + in_line, GROUP)),
            ):
                pl.semaphore_signal(barrier, inc=1, device_id=other, device_id_type=MESH)
        for load in loads[4:7]:
            load.start()
        for load in loads[7:]:
            load.start()
        load_raised(0).start()
        for load in loads[:4]:
            load.wait()

        attended = att_ref[...].T
        hidden = (
            feats_ref[...].astype(F32) + dg(attended, w_out_ref[...], 1, 0)
        ).astype(BF)
        hidden_s[...] = hidden
        local = parent_ref[...] - device_number() * CORE
        local = jnp.where(
            local < SPILL,
            local,
            jnp.where(local < CORE, local + SPILL, local - (CORE - SPILL)),
        )
        member = (local == iota((TABLE, ROWS), 0)) & (iota((TABLE, ROWS), 1) < live)
        member_f = jnp.where(member, 1.0, 0.0)
        counted = jnp.sum(member_f, axis=1, keepdims=True)
        sum_s[:, :C1] = dg(member_f.astype(BF), hidden, 1, 0)
        sum_s[:, C1 : 2 * C1] = dg(member_f.astype(BF), cot_ref[...], 1, 0)
        sum_s[:, 2 * C1 :] = jnp.broadcast_to(counted, (TABLE, HALF))
        for buf, rows in ((send_up, slice(SPILL, EDGE)), (send_down, slice(0, SPILL))):
            buf[:, : 2 * C1] = sum_s[rows, : 2 * C1].astype(BF)
            count = sum_s[rows, 2 * C1 :]
            high = count.astype(BF)
            low = (count - high.astype(F32)).astype(BF)
            buf[:, 2 * C1 :] = jnp.where(iota((SPILL, HALF), 1) < HALF // 2, high, low)
        pl.semaphore_wait(barrier, 2 * GROUP)
        for copy in near:
            copy.start()

        for load in loads[4:7]:
            load.wait()
        xhat, _ = norm_parts(feats_ref[...].astype(F32))
        normed = (xhat * gain_ref[...]).astype(BF)
        normed_s[...] = normed
        across_s[...] = normed.T
        values = dg(normed, w_qkv_ref[:, 2 * C1 :], 1, 0).astype(BF)
        ones = jnp.where(iota((ROWS, BAND), 1) < 2, 1.0, 0.0).astype(BF)
        for band in range(BANDS):
            values_s[band] = jnp.concatenate(
                [values[:, band * BAND : (band + 1) * BAND], ones], axis=1
            )
        for one in range(PAIR):
            cots_s[one] = jnp.zeros((HALF, ROWS), BF)
        column = jnp.broadcast_to(local.astype(F32), (HALF, ROWS)).T[:, :1].astype(jnp.int32)
        member = (column == iota((ROWS, TABLE), 1)) & (iota((ROWS, TABLE), 0) < live)
        member_s[...] = jnp.where(member, 1.0, 0.0).astype(BF)

        def coarse(total, total_cot, counted):
            inverse = 1.0 / jnp.maximum(counted, 1.0)
            pooled = (total * inverse).astype(BF)
            value, slope = gelu_and_slope(dg(pooled, w_down_ref[...], 1, 0))
            activ = value.astype(BF)
            back = dg(activ, w_up_ref[...], 1, 0).astype(BF)
            d_back = total_cot.astype(BF)
            d_pre = (dg(d_back, w_up_ref[...], 1, 1) * slope).astype(BF)
            share = dg(d_pre, w_down_ref[...], 1, 1) * inverse
            high = share.astype(BF)
            low = (share - high.astype(F32)).astype(BF)
            return pooled, activ, back, d_back, d_pre, high, low

        middle = slice(EDGE, TABLE)
        pooled, activ, back, d_back, d_pre, high, low = coarse(
            sum_s[middle, :C1],
            sum_s[middle, C1 : 2 * C1],
            sum_s[middle, 2 * C1 : 2 * C1 + 1],
        )
        back_s[middle, :] = back
        grad_up = dg(activ, d_back, 0, 0)
        grad_down = dg(pooled, d_pre, 0, 0)
        inner = member_s[:, middle]
        d_hidden_s[...] = (
            cot_ref[...].astype(F32) + dg(inner, high, 1, 0) + dg(inner, low, 1, 0)
        )

        for copy in near:
            copy.wait_recv()
        got = jnp.concatenate([recv_up[...], recv_down[...]], axis=0).astype(F32)
        count_in = (
            got[:, 2 * C1 : 2 * C1 + 1]
            + got[:, 2 * C1 + HALF // 2 : 2 * C1 + HALF // 2 + 1]
        )
        pooled, activ, back, d_back, d_pre, high, low = coarse(
            sum_s[:EDGE, :C1] + got[:, :C1],
            sum_s[:EDGE, C1 : 2 * C1] + got[:, C1 : 2 * C1],
            sum_s[:EDGE, 2 * C1 : 2 * C1 + 1] + count_in,
        )
        outer = member_s[:, :EDGE]
        d_hidden = (
            d_hidden_s[...]
            + dg(
                jnp.concatenate([outer, outer], axis=1),
                jnp.concatenate([high, low], axis=0),
                1,
                0,
            )
        )
        d_hidden_s[...] = d_hidden
        d_hidden_b = d_hidden.astype(BF)
        d_att_s[...] = dg(w_out_ref[...], d_hidden_b, 1, 1).astype(BF)
        back_s[:EDGE, :] = back
        grad_up = (grad_up + dg(activ[:SPILL], d_back[:SPILL], 0, 0)).astype(BF)
        grad_up = grad_up.reshape(GROUP, 2, 16, C1)
        grad_down = (grad_down + dg(pooled[:SPILL], d_pre[:SPILL], 0, 0)).astype(BF)
        grad_down = grad_down.reshape(GROUP, 16, C2)
        for core in range(2):
            e_data[core, :, :, :C1] = grad_up[:, core]
            e_data[core, :, :, C1 : 2 * C1] = grad_down[:, :, core * C1 : (core + 1) * C1]
        grad_out = dg(att_ref[...], d_hidden_b, 1, 0).astype(BF).reshape(GROUP, 16, C1)
        for core in range(2):
            e_data[core, :, :, 2 * C1 : GRADS_W] = grad_out[:, :, core * HALF : (core + 1) * HALF]
        for load in loads[7:]:
            load.wait()

    @pl.when(step < STEPS - 1)
    def _():
        load_raised(step + 1).start()

    load_raised(step).wait()

    def grad_columns(head, heads):
        rows = [
            d_proj_s[part * C1 + head * HD : part * C1 + (head + heads) * HD, :]
            for part in range(3)
        ]
        return dg(across_s[...], jnp.concatenate(rows, axis=0), 1, 1).astype(BF)

    def fill_halves(data, first, head, heads):
        grads = grad_columns(head, heads)
        width = 3 * heads * HD // 2
        for core in range(2):
            data[core, :, :, first : first + width] = grads[
                :, core * width : (core + 1) * width
            ].reshape(GROUP, 16, width)

    def serve(name, stage):
        if stage >= 0:
            chunks[name].advance(stage)
            return
        if name == "early":
            fill_halves(e_data, GRADS_W, 0, EARLY_HEADS)
        else:
            fill_halves(f_data, 0, EARLY_HEADS, LATE_HEADS)
        chunks[name].begin()

    band = step // (STEPS // BANDS)
    quarter = jnp.asarray(HD ** (-0.5), BF)
    for one in range(PAIR):
        for turn, name, stage in SERVICES:
            if turn % PAIR == one:
                @pl.when(step == turn // PAIR)
                def _(name=name, stage=stage):
                    serve(name, stage)

        head = step * PAIR + one
        start = pl.multiple_of(head * HD, HD)
        place = pl.multiple_of(lax.rem(head, BAND // HD) * HD, HD)
        cot = (d_att_s[pl.ds(start, HD), :].astype(F32) * scale_ref[head, :1, :]).astype(BF)
        inner = -jnp.sum(
            cot.astype(F32) * att_ref[pl.ds(start, HD), :].astype(F32), axis=0, keepdims=True
        )
        high = inner.astype(BF).astype(F32)
        rows = iota((HD, ROWS), 0)
        cots_s[one, :BAND, :] = jnp.zeros((BAND, ROWS), BF)
        cots_s[one, pl.ds(place, HD), :] = cot
        cots_s[one, BAND : BAND + HD, :] = jnp.where(
            rows == 0, high, jnp.where(rows == 1, inner - high, 0.0)
        ).astype(BF)
        raised = raised_s[lax.rem(step, 2), one]
        d_scores = raised * dg(values_s[band], cots_s[one], 1, 0).astype(BF)
        d_proj_s[pl.ds(start, HD), :] = dg(
            proj_ref[pl.ds(C1 + start, HD), :] * quarter, d_scores, 1, 0
        ).astype(BF)
        d_proj_s[pl.ds(2 * C1 + start, HD), :] = dg(cot, raised, 1, 1).astype(BF)
        d_proj_s[pl.ds(C1 + start, HD), :] = dg(
            proj_ref[pl.ds(start, HD), :] * quarter, d_scores, 1, 1
        ).astype(BF)

    @pl.when(step == STEPS - 1)
    def _():
        grads = grad_columns(EARLY_HEADS + LATE_HEADS, LAST_HEADS)
        t_data[...] = grads.reshape(GROUP, 16, LAST_W)
        last.begin()
        d_normed = dg(w_qkv_ref[...], d_proj_s[...], 1, 0).T
        early.advance(3)
        late.advance(1)
        xhat, inverse = norm_parts(feats_ref[...].astype(F32))
        grown = d_normed * gain_ref[...]
        along = jnp.mean(grown * xhat, axis=-1, keepdims=True)
        d_wide = inverse * (grown - jnp.mean(grown, axis=-1, keepdims=True) - xhat * along)
        d_feats_s[...] = (d_hidden_s[...] + d_wide).astype(BF)
        stores[1].start()
        last.advance(0)
        early.advance(4)
        stores[2].start()
        result_s[...] = (
            hidden_s[...].astype(F32) + dg(member_s[...], back_s[...], 1, 0)
        ).astype(BF)
        stores[0].start()
        late.advance(2)
        last.advance(1)
        late.advance(3)
        late.advance(4)
        stores[3].start()
        last.advance(2)
        stores[4].start()
        for chunk in (early, late, last):
            for stage in chunk.stages:
                stage.drain()
        for copy in near:
            copy.wait_send()
        for store in stores:
            store.wait()


def backward_call(counts, parent, gain, att, feats, w_out, cotangent, w_qkv, w_down, w_up,
                  proj, scale, raised):
    out = jax.ShapeDtypeStruct
    vmem = pltpu.VMEM
    anywhere = pl.BlockSpec(memory_space=pl.ANY)
    early, late, last = (
        (2, GROUP, 16, EARLY_W),
        (2, GROUP, 16, LATE_W),
        (GROUP, 16, LAST_W),
    )
    loaded = (att, feats, w_out, cotangent, w_qkv, w_down, w_up, proj, scale)

    def five(shape):
        return [
            vmem(shape, BF), vmem(shape, BF), vmem(shape[1:], BF), vmem(shape[1:], BF),
            vmem((8,) + shape[2:], BF), vmem(shape, BF),
        ]

    return pl.pallas_call(
        backward_kernel,
        grid=(STEPS,),
        in_specs=[
            pl.BlockSpec(memory_space=pltpu.SMEM),
            whole((1, ROWS)),
            whole((1, C1)),
        ]
        + [anywhere] * 10,
        out_specs=[anywhere] * 5,
        out_shape=[
            out((ROWS, C1), BF),
            out((ROWS, C1), BF),
            out(early, BF),
            out(late, BF),
            out(last, BF),
        ],
        scratch_shapes=[vmem(array.shape, array.dtype) for array in loaded]
        + [
            vmem((ROWS, C1), BF),
            vmem((ROWS, C1), BF),
            vmem((2, PAIR, ROWS, ROWS), BF),
            vmem((ROWS, C1), BF),
            vmem((TABLE, UP_W), F32),
            vmem((ROWS, C1), F32),
            vmem((ROWS, C1), BF),
            vmem((C1, ROWS), BF),
            vmem((C1, ROWS), BF),
            vmem((3 * C1, ROWS), BF),
            vmem((BANDS, ROWS, HALF), BF),
            vmem((PAIR, HALF, ROWS), BF),
            vmem((ROWS, TABLE), BF),
            vmem((TABLE, C1), BF),
            vmem((SPILL, UP_W), BF),
            vmem((SPILL, UP_W), BF),
            vmem((SPILL, UP_W), BF),
            vmem((SPILL, UP_W), BF),
        ]
        + five(early)
        + five(late)
        + [vmem(last, BF)] * 4
        + [
            pltpu.SemaphoreType.DMA((2,)),
            pltpu.SemaphoreType.DMA((2,)),
            pltpu.SemaphoreType.DMA((13,)),
            pltpu.SemaphoreType.DMA((13,)),
            pltpu.SemaphoreType.DMA((9,)),
            pltpu.SemaphoreType.DMA((2,)),
            pltpu.SemaphoreType.DMA((5,)),
        ],
        compiler_params=pltpu.CompilerParams(
            collective_id=0, has_side_effects=True, vmem_limit_bytes=58 * 2**20
        ),
        name="backward",
    )(counts, parent, gain, *loaded, raised)


def finish_kernel(
    result_hbm, d_feats_hbm, early_hbm, late_hbm, last_hbm,
    result_out, d_feats_out, qkv_out, out_out, down_out, up_out,
    result_s, d_feats_s, early_ref, late_ref, last_ref, qkv_s, out_s, down_s, up_s, load_sem, pass_sem, store_sem,
):
    loads = [
        pltpu.make_async_copy(src, dst, load_sem.at[n])
        for n, (src, dst) in enumerate(
            (
                (early_hbm, early_ref), (late_hbm, late_ref), (last_hbm, last_ref),
                (result_hbm, result_s), (d_feats_hbm, d_feats_s),
            )
        )
    ]
    passes = [
        pltpu.make_async_copy(result_s, result_out, pass_sem.at[0]),
        pltpu.make_async_copy(d_feats_s, d_feats_out, pass_sem.at[1]),
    ]
    stores = [
        pltpu.make_async_copy(src, dst, store_sem.at[n])
        for n, (src, dst) in enumerate(
            ((qkv_s, qkv_out), (out_s, out_out), (down_s, down_out), (up_s, up_out))
        )
    ]
    for load in loads[3:] + loads[:3]:
        load.start()
    for load, one in zip(loads[3:], passes):
        load.wait()
        one.start()
    loads[0].wait()
    for core in range(2):
        up_s[:, core] = early_ref[core, :, :, :C1].astype(F32)
        down_s[:, core * C1 : (core + 1) * C1] = (
            early_ref[core, :, :, C1 : 2 * C1].reshape(C1, C1).astype(F32)
        )
        out_s[:, core * HALF : (core + 1) * HALF] = (
            early_ref[core, :, :, 2 * C1 : GRADS_W].reshape(C1, HALF).astype(F32)
        )
    for store in stores[1:]:
        store.start()
    for load in loads[1:3]:
        load.wait()
    early, late = [
        jnp.concatenate(
            [ref[core, :, :, first:].astype(F32).reshape(C1, -1) for core in range(2)], axis=1
        )
        for ref, first in ((early_ref, GRADS_W), (late_ref, 0))
    ]
    last = last_ref[...].astype(F32).reshape(C1, LAST_W)
    for part in range(3):
        qkv_s[:, part * C1 : (part + 1) * C1] = jnp.concatenate(
            [
                piece[:, part * heads * HD : (part + 1) * heads * HD]
                for piece, heads in (
                    (early, EARLY_HEADS), (late, LATE_HEADS), (last, LAST_HEADS)
                )
            ],
            axis=1,
        )
    stores[0].start()
    for copy in passes + stores:
        copy.wait()


def finish_call(*parts):
    anywhere = pl.BlockSpec(memory_space=pl.ANY)
    shapes = [
        ((ROWS, C1), BF), ((ROWS, C1), BF), ((C1, 3 * C1), F32), ((C1, C1), F32),
        ((C1, C2), F32), ((GROUP, 2, 16, C1), F32),
    ]
    return pl.pallas_call(
        finish_kernel,
        in_specs=[anywhere] * 5,
        out_specs=[anywhere] * 6,
        out_shape=[jax.ShapeDtypeStruct(shape, kind) for shape, kind in shapes],
        scratch_shapes=[pltpu.VMEM(part.shape, BF) for part in parts]
        + [pltpu.VMEM(shape, F32) for shape, _ in shapes[2:]]
        + [
            pltpu.SemaphoreType.DMA((5,)),
            pltpu.SemaphoreType.DMA((2,)),
            pltpu.SemaphoreType.DMA((4,)),
        ],
        compiler_params=pltpu.CompilerParams(vmem_limit_bytes=60 * 2**20),
        name="finish",
    )(*parts)


def per_device(feats, counts, parent, ln_gain, w_qkv, w_out, w_down, w_up, cotangent):
    parent_row = parent.reshape(1, ROWS)
    gain = ln_gain.reshape(1, C1)
    raised, proj, scale, att = forward_call(counts, feats, gain, w_qkv)
    parts = backward_call(
        counts, parent_row, gain, att, feats, w_out, cotangent, w_qkv, w_down, w_up,
        proj, scale, raised,
    )
    result, d_feats, grad_qkv, grad_out, grad_down, grad_up = finish_call(*parts)
    return (result, d_feats, grad_qkv, grad_out, grad_down, grad_up.reshape(C2, C1))


def solution(mesh):
    rows = P(("pts", "grp"), None)
    line = P(("pts", "grp"))
    return jax.shard_map(
        per_device,
        mesh=mesh,
        in_specs=(rows, line, line, P(), P(), P(), P(), P(), rows),
        out_specs=(rows, rows, P(), P(), P(), P()),
        check_vma=False,
    )
```
